32 devices in a mesh: dp: 2 (over x), expert: 16 (over z, y, core).
Axes of the slice: x: 2, y: 2, z: 4, core: 2. Of those that a mesh axis runs over, the one named last changes fastest.
Arguments:
- hidden_in: bfloat16 [4096, 2048], P(('dp', 'expert')), may hold values from -6 to 6
- queries: bfloat16 [4096, 2048], P(('dp', 'expert')), may hold values from -150 to 150, as said below
- keys_values: bfloat16 [4096, 512], P(('dp', 'expert')), may hold values from -5 to 5
- segment_ids: int32 [2, 2048], P('dp', 'expert'), may hold values from 0 to 7, never falling along the last dimension, each value on 1 to 1024 neighbouring positions
- routes: int32 [4096, 8], P(('dp', 'expert')), may hold values from 0 to 15, all different within a row; in each aligned block of 128 rows (0 to 127, 128 to 255, ...) at most 96 rows name the same one
- gate_weights: float32 [4096, 8], P(('dp', 'expert')), may hold values from 0.05 to 1
- page_table: int32 [2, 128], P('dp'), may hold values from 0 to 127, each once within a row
- out_weight: bfloat16 [2048, 2048], P('dp'), may hold values from -0.125 to 0.125
- norm_gain: float32 [2048], replicated, may hold values from 0.1 to 1.9
- expert_gate: bfloat16 [16, 2048, 384], P('expert'), may hold values from -0.125 to 0.125
- expert_up: bfloat16 [16, 2048, 384], P('expert'), may hold values from -0.125 to 0.125
- expert_down: bfloat16 [16, 384, 2048], P('expert'), may hold values from -0.3125 to 0.3125
Outputs:
- hidden_out: bfloat16 [4096, 2048], P(('dp', 'expert'))
- cache_pages: bfloat16 [256, 16, 512], P(('dp', 'expert'))
The draws below stay inside these ranges and needn't reach their ends.
Inputs may be any that keep to these rules, and one draw needn't show every extreme that they name: `queries`: queries (hidden draw: some equal a multiple of their own key). `segment_ids`: within a pack numbers never fall; each prompt has 1 to 1024 tokens and some prompt has exactly 1024. `routes`: each row names 8 different experts; among the rows of one device no expert is named more than 96 times, a bound that some block reaches. `page_table`: each row is a permutation of its pack's 128 slots.
All inputs are finite; a program needn't handle non-finite values.
Results may differ from the reference program's by a relative error of at most 0.007.
Values may be sent and summed in bfloat16 or wider, within the bound.
No kernel may reach another device: no remote copies, remote signals or barrier semaphores. Data moves between devices by JAX's collectives and lax.ppermute only.
A program may use at most 128 MiB of HBM per device.

```python
import math
import jax
import jax.numpy as jnp
import numpy as np
from jax import lax

D = 2048
HD = 128
HQ = 16
HK = 2
FW = 384
TOP = 8
PAGE = 16
DOCS = 8
TOK_DEV = 128
EXPERTS = 16
PACK = 2048
TOKENS = 4096
MOST_LEN = 1024
PAGES = 128
CAP = 96
N_DP = 2
N_EXPERT = 16


def paired_draw(key):
    base_key = jax.random.fold_in(key, 1301)
    key_q, key_kv = jax.random.split(base_key, 2)
    queries = jnp.clip(jax.random.normal(key_q, (TOKENS, HQ * HD), jnp.float32), -6.0, 6.0)
    keys_values = jnp.clip(jax.random.normal(key_kv, (TOKENS, 2 * HK * HD), jnp.float32), -5.0, 5.0)
    return (queries, keys_values)


def draw_queries(key, part):
    return paired_draw(key)[0].astype(jnp.bfloat16)


def draw_keys_values(key, part):
    return paired_draw(key)[1].astype(jnp.bfloat16)


def block_levels(rng, extent, cuts, least, largest):
    def one(position, blocks):
        steps = jax.random.uniform(jax.random.fold_in(jax.random.fold_in(rng, 6), position), (blocks,), jnp.float32, least / len(cuts), largest / len(cuts))
        return jnp.repeat(jnp.exp(steps), extent[position] // blocks).reshape((-1,) + (1,) * (len(extent) - position - 1))

    loudness = one(*cuts[0])
    for cut in cuts[1:]:
        loudness = loudness * one(*cut)
    return loudness


def length_profile(amount, total, reach, slope):
    weights = [(1 << 20) // math.isqrt(standing ** slope) + 1 for standing in range(2, amount + 1)]
    rest, counts = total - reach - (amount - 1), [1] * (amount - 1)
    while rest > 0:
        free = [i for i in range(amount - 1) if counts[i] < reach]
        whole, remaining = sum([weights[i] for i in free]), rest
        for i in free:
            extra = min(reach - counts[i], max(1, remaining * weights[i] // whole), rest)
            counts[i] = counts[i] + extra
            rest = rest - extra
    return np.array([reach] + counts)


def ragged_sizes(own_key, count, total, bound, lean):
    if count == 2:
        one = jax.random.randint(own_key, (), max(1, total - bound), min(bound, total - 1) + 1)
        return jnp.stack([one, total - one])
    lengths = jnp.asarray(length_profile(count, total, bound, lean), jnp.int32)
    pairs = (count - 1) // 2
    donor, sink = lengths[1:1 + 2 * pairs:2], lengths[2:2 + 2 * pairs:2]
    room = jnp.minimum(donor - 1, bound - sink)
    moved = jax.random.randint(jax.random.fold_in(own_key, 1), (pairs,), 0, 1 << 20) % (room + 1)
    lengths = lengths.at[1:1 + 2 * pairs:2].set(donor - moved).at[2:2 + 2 * pairs:2].set(sink + moved)
    return lengths[jax.random.permutation(jax.random.fold_in(own_key, 2), count)]


def routed_block(rng, own, number, rows, count, top, bound, lean):
    sequence = jax.random.permutation(rng, count)
    packed, ordinary = load_shares(count, rows * top, bound, lean, True), load_shares(count, rows * top, bound, lean, False)
    places = jnp.arange(count)

    def named(lengths, offset_by):
        used = int((lengths > 0).sum())
        fixed = max(1, used // 4)
        moved = fixed + (places - fixed + offset_by * (used - fixed)) % max(1, count - fixed)
        return jnp.zeros((count,), jnp.int32).at[sequence[jnp.where(places < fixed, places, moved)]].set(jnp.asarray(lengths, jnp.int32))

    lengths = jnp.where(number % 4 == 0, named(packed, number // 4), named(ordinary, number - number // 4 - 1))
    mixed = jax.random.permutation(jax.random.fold_in(own, 3), count)
    giver, sink = mixed[0:count // 2 * 2:2], mixed[1:count // 2 * 2:2]
    margin = jnp.minimum(lengths[giver] - 1, bound - lengths[sink]) // 2
    margin = jnp.where((giver == sequence[0]) | (sink == sequence[0]) | (lengths[sink] == 0), 0, jnp.maximum(margin, 0))
    moved = jax.random.randint(jax.random.fold_in(own, 4), (count // 2,), 0, 1 << 20) % (margin + 1)
    lengths = lengths.at[giver].add(-moved).at[sink].add(moved)
    members = jnp.searchsorted(jnp.cumsum(lengths), jnp.arange(rows * top), side="right").astype(jnp.int32)
    table = members.reshape(top, rows).T
    table = table[jax.random.permutation(jax.random.fold_in(own, 1), rows)]
    offset_by = jax.random.randint(jax.random.fold_in(own, 2), (rows, 1), 0, top)
    return jnp.take_along_axis(table, (jnp.arange(top)[None, :] + offset_by) % top, axis=1)


def load_shares(amount, total, limit, slope, full):
    portions = [(1 << 20) // math.isqrt(grade ** slope) + 1 for grade in range(1, amount + 1)]
    largest = limit if full else min(limit, max(-(-total // amount), total * portions[0] // sum(portions)))
    least = 1 if total - largest >= amount - 1 else 0
    given, spare = [largest] + [least] * (amount - 1), total - largest - least * (amount - 1)
    while spare > 0:
        candidates = [i for i in range(1, amount) if given[i] < largest] or [i for i in range(1, amount) if given[i] < limit]
        pool, remaining = sum([portions[i] for i in candidates]), spare
        for i in candidates:
            addition = min(limit - given[i], max(1, remaining * portions[i] // pool), spare)
            given[i] = given[i] + addition
            spare = spare - addition
    return np.array(given)


def normal_values(stream_key, extent, width, limit, cuts=(), kind=jnp.bfloat16):
    drawn = jax.random.normal(stream_key, extent, jnp.float32) * width
    if len(cuts) > 0:
        drawn = block_levels(stream_key, extent, cuts, -0.22, 0.18) * drawn
    return jnp.clip(drawn, min=-limit, max=limit).astype(kind)


def setup_inputs(seed: int = 0) -> dict:
    splits = jax.random.split(jax.random.key(seed), 13)
    hidden_in = normal_values(splits[0], (TOKENS, D), 1.0, 6.0, ((0, 32),))
    queries = draw_queries(jax.random.fold_in(splits[12], 71), 0)
    keys_values = draw_keys_values(jax.random.fold_in(splits[12], 71), 0)
    segment_ids = jax.vmap(lambda own: jnp.searchsorted(jnp.cumsum(ragged_sizes(own, DOCS, PACK, MOST_LEN, 2)), jnp.arange(PACK), side="right"))(jax.random.split(splits[3], N_DP)).reshape((N_DP, PACK)).astype(jnp.int32)
    routes_keys = jax.random.split(jax.random.fold_in(splits[4], 1), TOKENS // TOK_DEV)
    routes_turns = jax.random.permutation(jax.random.fold_in(splits[4], 3), TOKENS // TOK_DEV)
    routes = jax.vmap(lambda own, number: routed_block(jax.random.fold_in(splits[4], 2), own, number, TOK_DEV, EXPERTS, TOP, CAP, 2))(routes_keys, routes_turns).reshape((TOKENS, TOP))
    gate_weights = jnp.clip(jnp.exp(math.log(1.0) - 2.9957323 * jax.random.uniform(splits[5], (TOKENS, TOP), jnp.float32) ** block_levels(splits[5], (TOKENS, TOP), ((0, 32),), -0.2, 0.2)), 0.05, 1.0)
    page_table = jax.vmap(lambda own: jax.random.permutation(own, PAGES))(jax.random.split(splits[6], N_DP)).reshape((N_DP, PAGES)).astype(jnp.int32)
    out_weight = normal_values(splits[7], (HQ * HD, D), (HQ * HD) ** -0.5, 0.125, ((0, 2),))
    norm_gain = jnp.clip(1.0 + 0.18 * jax.random.normal(splits[8], (D,), jnp.float32), 0.1, 1.9)
    expert_gate = normal_values(splits[9], (EXPERTS, D, FW), D ** -0.5, 0.125, ((0, 16),))
    expert_up = normal_values(splits[10], (EXPERTS, D, FW), D ** -0.5, 0.125, ((0, 16),))
    expert_down = normal_values(splits[11], (EXPERTS, FW, D), FW ** -0.5, 0.3125, ((0, 16),))
    return {"hidden_in": hidden_in, "queries": queries, "keys_values": keys_values, "segment_ids": segment_ids, "routes": routes, "gate_weights": gate_weights, "page_table": page_table, "out_weight": out_weight, "norm_gain": norm_gain, "expert_gate": expert_gate, "expert_up": expert_up, "expert_down": expert_down}


def reference(hidden_in, queries, keys_values, segment_ids, routes, gate_weights, page_table, out_weight, norm_gain, expert_gate, expert_up, expert_down):
    groups = HQ // HK
    kv_width = HK * HD
    packs_q = queries.reshape(N_DP, PACK, HK, groups, HD)
    packs_kv = keys_values.reshape(N_DP, PACK, 2 * kv_width)
    q_block = min(PACK, 512)
    block_total = PACK // q_block
    positions = jnp.arange(PACK, dtype=jnp.int32)

    def attend(index):
        pack_index = index // block_total
        first_row = index % block_total * q_block
        query_rows = lax.dynamic_slice_in_dim(packs_q[pack_index], first_row, q_block, 0).astype(jnp.float32)
        kv_rows = packs_kv[pack_index]
        key_rows = kv_rows[:, :kv_width].reshape(PACK, HK, HD).astype(jnp.float32)
        value_rows = kv_rows[:, kv_width:].reshape(PACK, HK, HD).astype(jnp.float32)
        segments_row = segment_ids[pack_index]
        query_seg = lax.dynamic_slice_in_dim(segments_row, first_row, q_block, 0)
        query_pos = first_row + jnp.arange(q_block, dtype=jnp.int32)
        allowed = (positions[None, :] <= query_pos[:, None]) & (segments_row[None, :] == query_seg[:, None])
        scores = jnp.einsum('thgd,shd->thgs', query_rows, key_rows) * (1.0 / math.sqrt(HD))
        masked = jnp.where(allowed[:, None, None, :], scores, -1e+30)
        row_top = lax.optimization_barrier(jnp.max(masked, axis=3, keepdims=True))
        probabilities = jnp.where(allowed[:, None, None, :], jnp.exp(masked - row_top), 0.0)
        denominator = lax.optimization_barrier(jnp.sum(probabilities, axis=3))
        rounded = lax.optimization_barrier(probabilities.astype(jnp.bfloat16)).astype(jnp.float32)
        heads_out = jnp.einsum('thgs,shd->thgd', rounded, value_rows) / denominator[..., None]
        return heads_out.reshape(q_block, HQ * HD).astype(jnp.bfloat16)
    attended = lax.map(attend, jnp.arange(N_DP * block_total, dtype=jnp.int32)).reshape(TOKENS, HQ * HD)
    projected = jnp.dot(attended, out_weight, preferred_element_type=jnp.float32)
    residual = hidden_in.astype(jnp.float32) + projected
    normed = (residual * lax.rsqrt(lax.optimization_barrier(jnp.mean(residual * residual, axis=1, keepdims=True)) + 1e-06) * norm_gain).astype(jnp.bfloat16)
    shares = gate_weights / lax.optimization_barrier(jnp.sum(gate_weights, axis=1, keepdims=True))
    row_limit = N_DP * N_EXPERT * CAP

    def per_expert(running, expert):
        chosen = routes == expert
        weight = lax.optimization_barrier(jnp.sum(jnp.where(chosen, shares, 0.0), axis=1))
        routed = jnp.any(chosen, axis=1)
        row_index = jnp.nonzero(routed, size=row_limit, fill_value=0)[0].astype(jnp.int32)
        filled = jnp.arange(row_limit, dtype=jnp.int32) < jnp.sum(routed.astype(jnp.int32))
        inputs = normed[row_index]
        gate_value = jnp.dot(inputs, expert_gate[expert], preferred_element_type=jnp.float32)
        up_value = jnp.dot(inputs, expert_up[expert], preferred_element_type=jnp.float32)
        hidden_units = (jax.nn.silu(gate_value) * up_value).astype(jnp.bfloat16)
        result = lax.optimization_barrier(jnp.dot(hidden_units, expert_down[expert], preferred_element_type=jnp.float32).astype(jnp.bfloat16)).astype(jnp.float32)
        scaled = jnp.where(filled, weight[row_index], 0.0)
        return (running.at[row_index].add(result * scaled[:, None]), None)
    combined, _ = lax.scan(per_expert, jnp.zeros((TOKENS, D), jnp.float32), jnp.arange(EXPERTS, dtype=jnp.int32))
    hidden_out = (residual + combined).astype(jnp.bfloat16)
    page_rows = keys_values.reshape(N_DP * PAGES, PAGE, 2 * kv_width)
    slot_index = (page_table + PAGES * jnp.arange(N_DP, dtype=jnp.int32)[:, None]).reshape(-1).astype(jnp.int32)
    cache_pages = jnp.zeros((N_DP * PAGES, PAGE, 2 * kv_width), jnp.bfloat16).at[slot_index].set(page_rows)
    return (hidden_out, cache_pages)
```

```python
import functools
import math

import jax
import jax.numpy as jnp
from jax import lax
from jax.experimental import pallas as pl
from jax.experimental.pallas import tpu as pltpu
from jax.sharding import PartitionSpec as P

HD = 128
HQ = 16
HK = 2
TOP = 8
PAGE = 16
LANES = 128
KEY_BLOCK = 256

neg_big = -1e30
norm_eps = 1e-06

ROUTE_LANE = 8
HIGH_LANE = 16
LOW_LANE = 24

VMEM_LIMIT = 48 * 1024 * 1024

vmem_spec = pl.BlockSpec(memory_space=pltpu.VMEM)
smem_spec = pl.BlockSpec(memory_space=pltpu.SMEM)
any_spec = pl.BlockSpec(memory_space=pl.ANY)


def lane_sum(values):
    return jnp.sum(values, axis=1, keepdims=True)


def pack_kernel(kv_ref, seg_ref, routes_ref, weights_ref, out_ref):
    rows, kv_cols = kv_ref.shape
    out_ref[:, :kv_cols] = kv_ref[...]
    row_id = lax.broadcasted_iota(jnp.int32, (rows, rows), 0)
    col_id = lax.broadcasted_iota(jnp.int32, (rows, rows), 1)
    seg = seg_ref[...].astype(jnp.float32)
    seg_col = lane_sum(jnp.where(row_id == col_id, seg, 0.0))
    weights = weights_ref[...]
    shares = weights / lane_sum(weights)
    high = shares.astype(jnp.bfloat16).astype(jnp.float32)
    low = shares - high
    routes = routes_ref[...].astype(jnp.float32)
    lane = lax.broadcasted_iota(jnp.int32, (rows, LANES), 1)
    aux = jnp.where(lane == 0, seg_col, 0.0)
    for k in range(TOP):
        aux = jnp.where(lane == ROUTE_LANE + k, routes[:, k : k + 1], aux)
        aux = jnp.where(lane == HIGH_LANE + k, high[:, k : k + 1], aux)
        aux = jnp.where(lane == LOW_LANE + k, low[:, k : k + 1], aux)
    out_ref[:, kv_cols:] = aux.astype(jnp.bfloat16)


def attend_kernel(shape, pos_ref, pages_ref, q_ref, *refs):
    nz, ny, nc = shape
    count = nz * ny * nc
    shards = refs[:count]
    out_ref, cache_ref, aux_ref = refs[count : count + 3]
    held, q_rows, top, total, acc, sems = refs[count + 3 :]
    tok_rows = q_ref.shape[0]
    kv_width = HK * HD
    member, z, y, c = pos_ref[0], pos_ref[1], pos_ref[2], pos_ref[3]
    copies = []
    for i in range(count):
        kz, ky, kc = i // (ny * nc), i // nc % ny, i % nc
        shard = ((z ^ kz) * ny + (y ^ ky)) * nc + (c ^ kc)
        start = pl.multiple_of(shard * tok_rows, tok_rows)
        copy = pltpu.make_async_copy(shards[i], held.at[pl.ds(start, tok_rows)], sems.at[i])
        copy.start()
        copies.append(copy)
    for h in range(HQ):
        q_rows[h * tok_rows : (h + 1) * tok_rows, :] = q_ref[:, h * HD : (h + 1) * HD]
    top[...] = jnp.full(top.shape, neg_big, jnp.float32)
    total[...] = jnp.zeros(total.shape, jnp.float32)
    acc[...] = jnp.zeros(acc.shape, jnp.float32)
    for copy in copies:
        copy.wait()
    lane = lax.broadcasted_iota(jnp.int32, (tok_rows, LANES), 1).astype(jnp.float32)

    def count_lower(s, below):
        start = pl.multiple_of(s * tok_rows, tok_rows)
        aux = held[pl.ds(start, tok_rows), 2 * kv_width :]
        aux_ref[pl.ds(start, tok_rows), :] = aux
        seg = aux[:, 0:1].astype(jnp.float32)
        return below + jnp.where(seg < lane, 1.0, 0.0)

    below = lax.fori_loop(0, count, count_lower, jnp.zeros((tok_rows, LANES), jnp.float32))
    below = jnp.sum(below, axis=0, keepdims=True)
    first_row = pl.multiple_of(member * tok_rows, tok_rows)
    own_seg = held[pl.ds(first_row, tok_rows), 2 * kv_width :][:, 0:1].astype(jnp.float32)
    seg_start = lane_sum(jnp.where(own_seg == lane, below, 0.0)).astype(jnp.int32)
    query_pos = first_row + lax.broadcasted_iota(jnp.int32, (tok_rows, 1), 0)
    last_block = first_row // KEY_BLOCK
    first_block = jnp.min(seg_start) // KEY_BLOCK
    scale = 1.0 / math.sqrt(HD)
    unit = 2 * tok_rows
    groups = HQ // HK

    def attend(step, carried):
        base = pl.multiple_of((last_block - step) * KEY_BLOCK, KEY_BLOCK)
        key_pos = base + lax.broadcasted_iota(jnp.int32, (tok_rows, KEY_BLOCK), 1)
        seen = (key_pos >= seg_start) & (key_pos <= query_pos)
        bias = jnp.where(seen, 0.0, neg_big)
        bias = jnp.concatenate([bias, bias], axis=0)
        for g in range(HK):
            key = held[pl.ds(base, KEY_BLOCK), g * HD : (g + 1) * HD]
            value = held[pl.ds(base, KEY_BLOCK), kv_width + g * HD : kv_width + (g + 1) * HD]
            for u in range(groups // 2):
                rows = pl.ds((g * groups + 2 * u) * tok_rows, unit)
                scores = lax.dot_general(
                    q_rows[rows, :],
                    key,
                    (((1,), (1,)), ((), ())),
                    preferred_element_type=jnp.float32,
                )
                scores = scores + bias
                old_top = top[rows, :]
                new_top = jnp.maximum(old_top, jnp.max(scores, axis=1, keepdims=True))
                weights = jnp.exp((scores - new_top) * scale)
                factor = jnp.exp((old_top - new_top) * scale)
                top[rows, :] = new_top
                total[rows, :] = total[rows, :] * factor + lane_sum(weights)
                acc[rows, :] = acc[rows, :] * factor + jnp.dot(
                    weights.astype(jnp.bfloat16), value, preferred_element_type=jnp.float32
                )
        return carried

    lax.fori_loop(0, last_block - first_block + 1, attend, 0)
    for h in range(HQ):
        rows = slice(h * tok_rows, (h + 1) * tok_rows)
        out_ref[:, h * HD : (h + 1) * HD] = (acc[rows, :] / total[rows, :]).astype(jnp.bfloat16)
    for s in range(cache_ref.shape[0]):
        start = pl.multiple_of(pages_ref[s] * PAGE, PAGE)
        cache_ref[s] = held[pl.ds(start, PAGE), : 2 * kv_width]


def project_kernel(offsets, pos_ref, att_ref, hidden_ref, gain_ref, *refs):
    count = len(offsets)
    pieces = refs[:count]
    residual_ref, normed_ref, weight, sems = refs[count:]
    rows, width = hidden_ref.shape
    copies = []
    for i in range(count):
        piece_rows = pieces[i].shape[0]
        start = pl.multiple_of(offsets[i](pos_ref), LANES)
        copy = pltpu.make_async_copy(pieces[i], weight.at[pl.ds(start, piece_rows)], sems.at[i])
        copy.start()
        copies.append(copy)
    for copy in copies:
        copy.wait()
    step = 512
    squares = jnp.zeros((rows, 1), jnp.float32)
    for n in range(0, width, step):
        projected = jnp.dot(
            att_ref[...], weight[:, n : n + step], preferred_element_type=jnp.float32
        )
        part = hidden_ref[:, n : n + step].astype(jnp.float32) + projected
        residual_ref[:, n : n + step] = part
        squares = squares + lane_sum(part * part)
    factor = lax.rsqrt(squares / width + norm_eps)
    normed_ref[...] = (residual_ref[...] * factor * gain_ref[...]).astype(jnp.bfloat16)


def expert_kernel(items, shape, pos_ref, aux_ref, *refs):
    nz, ny, nc = shape
    n_sources = sum(len(sources) for _, sources in items)
    sources = refs[:n_sources]
    weights = refs[n_sources : n_sources + 6]
    outs = refs[n_sources + 6 : n_sources + 6 + len(items)]
    x, aux, first, second, down, inner, x_sems, aux_sems, w_sems = refs[n_sources + 6 + len(items) :]
    member, z, y, c = pos_ref[0], pos_ref[1], pos_ref[2], pos_ref[3]
    rows = outs[0].shape[0]
    width = first.shape[1]
    hidden = first.shape[2]
    waits = []
    base = 0
    for i, (ky, table) in enumerate(items):
        block = pl.ds(i * rows, rows)
        for name in sorted(table):
            place = sorted(table).index(name)
            for at_z, far in table[name]:
                source = sources[base + place]
                shard = ((at_z + far) * ny + (y ^ ky)) * nc + c

                @pl.when(z == at_z)
                def _():
                    pltpu.make_async_copy(source, x.at[block], x_sems.at[i]).start()
                    start = pl.multiple_of(shard * rows, rows)
                    pltpu.make_async_copy(
                        aux_ref.at[pl.ds(start, rows)], aux.at[block], aux_sems.at[i]
                    ).start()

        waits.append(pltpu.make_async_copy(sources[base], x.at[block], x_sems.at[i]))
        waits.append(
            pltpu.make_async_copy(aux_ref.at[pl.ds(0, rows)], aux.at[block], aux_sems.at[i])
        )
        base += len(table)
    targets = (
        first.at[0],
        second.at[0],
        first.at[1],
        second.at[1],
        down.at[pl.ds(0, hidden)],
        down.at[pl.ds(hidden, hidden)],
    )
    loads = []
    for i in range(6):
        load = pltpu.make_async_copy(weights[i], targets[i], w_sems.at[i])
        load.start()
        loads.append(load)
    for wait in waits:
        wait.wait()
    extra = aux[...].astype(jnp.float32)
    lane = lax.broadcasted_iota(jnp.int32, extra.shape, 1)
    is_high = (lane >= HIGH_LANE) & (lane < HIGH_LANE + TOP)
    named = pltpu.roll(extra, HIGH_LANE - ROUTE_LANE, 1)
    share = extra + pltpu.roll(extra, LANES - (LOW_LANE - HIGH_LANE), 1)
    for e in range(2):
        expert = (member ^ e).astype(jnp.float32)
        chosen = lane_sum(jnp.where(is_high & (named == expert), share, 0.0))
        loads[2 * e].wait()
        loads[2 * e + 1].wait()
        gate = jnp.dot(x[...], first[e], preferred_element_type=jnp.float32)
        up = jnp.dot(x[...], second[e], preferred_element_type=jnp.float32)
        inner[:, e * hidden : (e + 1) * hidden] = (
            gate * jax.nn.sigmoid(gate) * up * chosen
        ).astype(jnp.bfloat16)
    loads[4].wait()
    loads[5].wait()
    step = 512
    for n in range(0, width, step):
        result = jnp.dot(inner[...], down[:, n : n + step], preferred_element_type=jnp.float32)
        for i in range(len(items)):
            outs[i][:, n : n + step] = result[i * rows : (i + 1) * rows].astype(jnp.bfloat16)


def arrival_slots(nz):
    table = []
    for z in range(nz):
        slots = [0] + [None] * (nz - 1)
        left = []
        for far in range(1, nz):
            both = [s for s in (far, -far) if 0 <= z + s < nz]
            if z >= nz // 2:
                both = both[::-1]
            if both:
                slots[far] = both.pop()
            left += both
        for k in range(1, nz):
            if slots[k] is None:
                slots[k] = left.pop()
        table.append(slots)
    return table


def body(
    dims,
    hidden_in,
    queries,
    keys_values,
    segment_ids,
    routes,
    gate_weights,
    page_table,
    out_weight,
    norm_gain,
    expert_gate,
    expert_up,
    expert_down,
):
    n_dp, nz, ny, nc = dims
    shape = (nz, ny, nc)
    members = nz * ny * nc
    tok_rows, width = hidden_in.shape
    member = lax.axis_index("expert")
    side = lax.axis_index("dp")
    z, y, c = member // (ny * nc), member // nc % ny, member % nc
    position = jnp.stack([member, z, y, c, side]).astype(jnp.int32)
    params = pltpu.CompilerParams(vmem_limit_bytes=VMEM_LIMIT)

    def at(zz, yy, cc):
        return (zz * ny + yy) * nc + cc

    places = [(a, b, d) for a in range(nz) for b in range(ny) for d in range(nc)]

    def flip(array, kz, ky, kc):
        pairs = [(at(a, b, d), at(a ^ kz, b ^ ky, d ^ kc)) for a, b, d in places]
        return lax.ppermute(array, "expert", pairs)

    def shift(array, by, senders):
        pairs = [(at(a, b, d), at(a + by, b, d)) for a, b, d in places if a in senders]
        return lax.ppermute(array, "expert", pairs)

    def flip_y(array, ky, keep):
        pairs = [(at(a, b, d), at(a, b ^ ky, d)) for a, b, d in places if a in keep]
        return lax.ppermute(array, "expert", pairs)

    kv_cols = keys_values.shape[1]
    packed = pl.pallas_call(
        pack_kernel,
        out_shape=jax.ShapeDtypeStruct((tok_rows, kv_cols + LANES), jnp.bfloat16),
        in_specs=[vmem_spec] * 4,
        out_specs=vmem_spec,
    )(keys_values, segment_ids.reshape(1, tok_rows), routes, gate_weights)
    shards = {}
    for kz in range(nz):
        along = packed if kz == 0 else flip(packed, kz, 0, 0)
        for ky in range(ny):
            across = along if ky == 0 else flip(along, 0, ky, 0)
            shards[kz, ky, 0] = across
            for kc in range(1, nc):
                shards[kz, ky, kc] = flip(across, 0, 0, kc)
    shard_list = [shards[place] for place in places]

    half = out_weight.shape[0]
    if n_dp == 2 and ny == 2 and half % (8 * LANES) == 0:
        quarter = half // 4
        part = quarter // nc
        swap = [(0, 1), (1, 0)]

        def send_rows(start):
            rows = lax.dynamic_slice_in_dim(out_weight, start + c * part, part, 0)
            return lax.ppermute(rows, "dp", swap)

        def from_other(start, kc):
            return lambda pos: (1 - pos[4]) * half + start(pos) + (pos[3] ^ kc) * part

        got = [send_rows(y * quarter), None, send_rows(2 * quarter), send_rows(3 * quarter)]
        got[1] = flip(got[0], 0, 1, 0)
        starts = [
            lambda pos: pos[2] * quarter,
            lambda pos: (1 - pos[2]) * quarter,
            lambda pos: 2 * quarter,
            lambda pos: 3 * quarter,
        ]
        pieces = [out_weight]
        offsets = [lambda pos: pos[4] * half]
        for piece, start in zip(got, starts):
            pieces += [piece, flip(piece, 0, 0, 1)]
            offsets += [from_other(start, 0), from_other(start, 1)]
    else:
        pieces = [lax.all_gather(out_weight, "dp", axis=0, tiled=True)]
        offsets = [lambda pos: 0]
    own = [expert_gate[0], expert_up[0], expert_down[0]]
    other = [flip(array, 0, 0, 1) for array in own]
    experts = [own[0], own[1], other[0], other[1], own[2], other[2]]

    table_row = page_table.reshape(-1)
    slot_count = tok_rows // PAGE
    slot_ids = member * slot_count + jnp.arange(slot_count, dtype=jnp.int32)
    matches = (table_row[None, :] == slot_ids[:, None]).astype(jnp.int32)
    page_ids = jnp.arange(table_row.shape[0], dtype=jnp.int32)
    page_of_slot = jnp.sum(matches * page_ids[None, :], axis=1)
    attended, cache_pages, aux = pl.pallas_call(
        functools.partial(attend_kernel, shape),
        out_shape=(
            jax.ShapeDtypeStruct((tok_rows, HQ * HD), jnp.bfloat16),
            jax.ShapeDtypeStruct((slot_count, PAGE, kv_cols), jnp.bfloat16),
            jax.ShapeDtypeStruct((members * tok_rows, LANES), jnp.bfloat16),
        ),
        in_specs=[smem_spec, smem_spec, vmem_spec] + [any_spec] * members,
        out_specs=(vmem_spec, vmem_spec, vmem_spec),
        scratch_shapes=[
            pltpu.VMEM((members * tok_rows, kv_cols + LANES), jnp.bfloat16),
            pltpu.VMEM((HQ * tok_rows, HD), jnp.bfloat16),
            pltpu.VMEM((HQ * tok_rows, 1), jnp.float32),
            pltpu.VMEM((HQ * tok_rows, 1), jnp.float32),
            pltpu.VMEM((HQ * tok_rows, HD), jnp.float32),
            pltpu.SemaphoreType.DMA((members,)),
        ],
        compiler_params=params,
    )(position, page_of_slot, queries, *shard_list)

    residual, normed = pl.pallas_call(
        functools.partial(project_kernel, offsets),
        out_shape=(
            jax.ShapeDtypeStruct((tok_rows, width), jnp.float32),
            jax.ShapeDtypeStruct((tok_rows, width), jnp.bfloat16),
        ),
        in_specs=[smem_spec, vmem_spec, vmem_spec, vmem_spec] + [any_spec] * len(pieces),
        out_specs=(vmem_spec, vmem_spec),
        scratch_shapes=[
            pltpu.VMEM((HQ * HD, width), jnp.bfloat16),
            pltpu.SemaphoreType.DMA((len(pieces),)),
        ],
        compiler_params=params,
    )(position, attended, hidden_in, norm_gain.reshape(1, width), *pieces)

    here = {0: normed}
    for far in range(1, nz):
        here[-far] = shift(here[1 - far], 1, range(far - 1, nz - 1))
        here[far] = shift(here[far - 1], -1, range(1, nz - far + 1))
    planes = [here]
    for ky in range(1, ny):
        planes.append(
            {
                far: flip_y(here[far], ky, [a for a in range(nz) if 0 <= a + far < nz])
                for far in here
            }
        )
    slots = arrival_slots(nz)

    def item_table(k):
        table = {}
        for a in range(nz):
            table.setdefault(slots[a][k], []).append((a, slots[a][k]))
        return table

    results = {}
    hidden = expert_gate.shape[2]
    for call in range(nz + 1):
        chosen = [(k, ky) for k in range(nz) for ky in range(ny) if k + (ky > 0) == call]
        items = [(ky, item_table(k)) for k, ky in chosen]
        sources = [planes[ky][far] for ky, table in items for far in sorted(table)]
        rows = len(items) * tok_rows
        outs = pl.pallas_call(
            functools.partial(expert_kernel, items, shape),
            out_shape=[jax.ShapeDtypeStruct((tok_rows, width), jnp.bfloat16)] * len(items),
            in_specs=[smem_spec] + [any_spec] * (len(sources) + 7),
            out_specs=[vmem_spec] * len(items),
            scratch_shapes=[
                pltpu.VMEM((rows, width), jnp.bfloat16),
                pltpu.VMEM((rows, LANES), jnp.bfloat16),
                pltpu.VMEM((2, width, hidden), jnp.bfloat16),
                pltpu.VMEM((2, width, hidden), jnp.bfloat16),
                pltpu.VMEM((2 * hidden, width), jnp.bfloat16),
                pltpu.VMEM((rows, 2 * hidden), jnp.bfloat16),
                pltpu.SemaphoreType.DMA((len(items),)),
                pltpu.SemaphoreType.DMA((len(items),)),
                pltpu.SemaphoreType.DMA((6,)),
            ],
            compiler_params=params,
            cost_estimate=pl.CostEstimate(
                flops=12 * rows * width * hidden,
                bytes_accessed=12 * width * hidden,
                transcendentals=0,
            ),
        )(position, aux, *sources, *experts)
        for key, value in zip(chosen, outs):
            results[key] = value

    def as_float(array):
        return array.astype(jnp.float32)

    sums = {}
    for k in range(nz - 1, -1, -1):
        sums[k] = as_float(results[k, 0])
        for ky in range(1, ny):
            sums[k] = sums[k] + as_float(flip(results[k, ky], 0, ky, 0))

    def sum_for(far):
        holders = {}
        for a in range(nz):
            if 0 <= a + far < nz:
                holders.setdefault(slots[a].index(far), []).append(a)
        picked = None
        for k, zs in holders.items():
            if picked is None:
                picked = sums[k]
            else:
                mine = functools.reduce(jnp.logical_or, [z == a for a in zs])
                picked = jnp.where(mine, sums[k], picked)
        return picked

    from_below = from_above = None
    for step in range(1, nz):
        far = nz - step
        upward, downward = sum_for(far), sum_for(-far)
        if step > 1:
            upward = upward + as_float(from_below)
            downward = downward + as_float(from_above)
        from_below = shift(upward.astype(jnp.bfloat16), 1, range(0, step))
        from_above = shift(downward.astype(jnp.bfloat16), -1, range(nz - step, nz))
    combined = sums[0] + as_float(from_below) + as_float(from_above)
    hidden_out = (residual + combined).astype(jnp.bfloat16)
    return (hidden_out, cache_pages)


def split_axis(mesh):
    n_dp = mesh.shape["dp"]
    members = mesh.shape["expert"]
    nc = 2
    ny = n_dp if members % (nc * n_dp) == 0 else 1
    return (n_dp, members // (nc * ny), ny, nc)


def solution(mesh):
    return jax.shard_map(
        functools.partial(body, split_axis(mesh)),
        mesh=mesh,
        in_specs=(
            P(("dp", "expert"), None),
            P(("dp", "expert"), None),
            P(("dp", "expert"), None),
            P("dp", "expert"),
            P(("dp", "expert"), None),
            P(("dp", "expert"), None),
            P("dp", None),
            P("dp", None),
            P(),
            P("expert", None, None),
            P("expert", None, None),
            P("expert", None, None),
        ),
        out_specs=(P(("dp", "expert"), None), P(("dp", "expert"), None, None)),
        check_vma=False,
    )
```

```python
import functools
import math

import jax
import jax.numpy as jnp
from jax import lax
from jax.experimental import pallas as pl
from jax.experimental.pallas import tpu as pltpu
from jax.sharding import PartitionSpec as P

HD = 128
HQ = 16
HK = 2
TOP = 8
PAGE = 16
LANES = 128
KEY_BLOCK = 256

neg_big = -1e30
norm_eps = 1e-06

ROUTE_LANE = 8
HIGH_LANE = 16
LOW_LANE = 24

VMEM_LIMIT = 60 * 1024 * 1024
FFN_FLOPS = 10**6
ATT_FLOPS = 10**6

vmem_spec = pl.BlockSpec(memory_space=pltpu.VMEM)
smem_spec = pl.BlockSpec(memory_space=pltpu.SMEM)
any_spec = pl.BlockSpec(memory_space=pltpu.HBM)


def own_place(shape):
    _, ny, nc = shape
    member = lax.axis_index("expert")
    return member, member // (ny * nc), member // nc % ny, member % nc, lax.axis_index("dp")


def lane_sum(values):
    return jnp.sum(values, axis=1, keepdims=True)


def pack_kernel(kv_ref, seg_ref, routes_ref, weights_ref, out_ref):
    rows, kv_cols = kv_ref.shape
    out_ref[:, :kv_cols] = kv_ref[...]
    row_id = lax.broadcasted_iota(jnp.int32, (rows, rows), 0)
    col_id = lax.broadcasted_iota(jnp.int32, (rows, rows), 1)
    identity = jnp.where(row_id == col_id, 1.0, 0.0).astype(jnp.bfloat16)
    weights = weights_ref[...]
    shares = weights / jnp.sum(weights, axis=0, keepdims=True)
    high = shares.astype(jnp.bfloat16).astype(jnp.float32)
    seg = jnp.broadcast_to(seg_ref[...].astype(jnp.float32), (ROUTE_LANE, rows))
    lines = [seg, routes_ref[...].astype(jnp.float32), high, shares - high]
    lines.append(jnp.zeros((LANES - LOW_LANE - TOP, rows), jnp.float32))
    lines = jnp.concatenate(lines, axis=0).astype(jnp.bfloat16)
    turned = lax.dot_general(
        identity, lines, (((1,), (1,)), ((), ())), preferred_element_type=jnp.float32
    )
    out_ref[:, kv_cols:] = turned.astype(jnp.bfloat16)


def turn_kernel(q_ref, out_ref):
    rows = q_ref.shape[0]
    for h in range(HQ):
        part = q_ref[:, h * HD : (h + 1) * HD].astype(jnp.float32)
        out_ref[:, h * rows : (h + 1) * rows] = part.T.astype(jnp.bfloat16)


def attend_kernel(shape, own_part, table_ref, seg_ref, q_ref, hidden_ref, weight_ref, *refs):
    nz, ny, nc = shape
    count = nz * ny * nc
    shards = refs[:count]
    out_ref, partial_ref, cache_ref, aux_ref = refs[count : count + 4]
    held, top, total, acc, attended, weight, pages, sems, more_sems = refs[count + 4 :]
    tok_rows, width = hidden_ref.shape
    kv_width = HK * HD
    member, z, y, c, side = own_place(shape)
    copies = []
    for i in range(count):
        kz, ky, kc = i // (ny * nc), i // nc % ny, i % nc
        shard = ((z ^ kz) * ny + (y ^ ky)) * nc + (c ^ kc)
        start = pl.multiple_of(shard * tok_rows, tok_rows)
        copy = pltpu.make_async_copy(shards[i], held.at[pl.ds(start, tok_rows)], sems.at[i])
        copy.start()
        copies.append(copy)
    weight_copy = pltpu.make_async_copy(weight_ref, weight, more_sems.at[0])
    if own_part:
        weight_copy.start()
    top[...] = jnp.full(top.shape, neg_big, jnp.float32)
    total[...] = jnp.zeros(total.shape, jnp.float32)
    acc[...] = jnp.zeros(acc.shape, jnp.float32)
    slots = cache_ref.shape[0]

    def find_slot(page, carried):
        slot = table_ref[0, page] - member * slots

        @pl.when((slot >= 0) & (slot < slots))
        def _():
            pages[slot] = page

        return carried

    lax.fori_loop(0, table_ref.shape[1], find_slot, 0, unroll=8)
    for copy in copies:
        copy.wait()
    later = [pltpu.make_async_copy(held.at[:, 2 * kv_width :], aux_ref, more_sems.at[1])]
    for s in range(slots):
        start = pl.multiple_of(pages[s] * PAGE, PAGE)
        page = held.at[pl.ds(start, PAGE), pl.ds(0, 2 * kv_width)]
        later.append(pltpu.make_async_copy(page, cache_ref.at[s], more_sems.at[2 + s]))
    for copy in later:
        copy.start()
    own_seg = seg_ref[...].astype(jnp.float32)

    def count_lower(s, below):
        start = pl.multiple_of(s * tok_rows, tok_rows)
        seg = held[pl.ds(start, tok_rows), 2 * kv_width :][:, 0:1].astype(jnp.float32)
        return below + jnp.where(seg < own_seg, 1.0, 0.0)

    below = lax.fori_loop(0, member + 1, count_lower, jnp.zeros((tok_rows, tok_rows), jnp.float32))
    seg_start = jnp.sum(below, axis=0, keepdims=True).astype(jnp.int32)
    first_row = member * tok_rows
    query_pos = first_row + lax.broadcasted_iota(jnp.int32, (1, tok_rows), 1)
    last_block = first_row // KEY_BLOCK
    first_block = jnp.min(seg_start) // KEY_BLOCK
    scale = 1.0 / math.sqrt(HD)
    heads = 4
    cols = heads * tok_rows
    groups = HQ // HK

    def attend(step, carried):
        base = pl.multiple_of((last_block - step) * KEY_BLOCK, KEY_BLOCK)
        key_pos = base + lax.broadcasted_iota(jnp.int32, (KEY_BLOCK, tok_rows), 0)
        seen = (key_pos >= seg_start) & (key_pos <= query_pos)
        bias = jnp.where(seen, 0.0, neg_big)
        bias = jnp.concatenate([bias] * heads, axis=1)
        for g in range(HK):
            key = held[pl.ds(base, KEY_BLOCK), g * HD : (g + 1) * HD]
            value = held[pl.ds(base, KEY_BLOCK), kv_width + g * HD : kv_width + (g + 1) * HD]
            for u in range(0, groups, heads):
                unit = slice((g * groups + u) * tok_rows, (g * groups + u) * tok_rows + cols)
                scores = jnp.dot(key, q_ref[:, unit], preferred_element_type=jnp.float32) + bias
                old_top = top[:, unit]
                new_top = jnp.maximum(old_top, jnp.max(scores, axis=0, keepdims=True))
                weights = jnp.exp((scores - new_top) * scale)
                factor = jnp.exp((old_top - new_top) * scale)
                top[:, unit] = new_top
                total[:, unit] = total[:, unit] * factor + jnp.sum(weights, axis=0, keepdims=True)
                added = lax.dot_general(
                    value,
                    weights.astype(jnp.bfloat16),
                    (((0,), (0,)), ((), ())),
                    preferred_element_type=jnp.float32,
                )
                acc[:, unit] = acc[:, unit] * factor + added
        return carried

    lax.fori_loop(0, last_block - first_block + 1, attend, 0)
    for h in range(HQ):
        unit = slice(h * tok_rows, (h + 1) * tok_rows)
        head = acc[:, unit] / total[:, unit]
        attended[:, h * HD : (h + 1) * HD] = head.T.astype(jnp.bfloat16)
    step = 512
    if own_part:
        half = weight.shape[0]
        mine = attended[:, pl.ds(pl.multiple_of(side * half, half), half)]
        out_ref[...] = attended[:, pl.ds(pl.multiple_of((1 - side) * half, half), half)]
        weight_copy.wait()
        for n in range(0, width, step):
            part = slice(n, n + step)
            partial_ref[:, part] = hidden_ref[:, part].astype(jnp.float32) + jnp.dot(
                mine, weight[:, part], preferred_element_type=jnp.float32
            )
    else:
        out_ref[...] = attended[...]
        partial_ref[...] = hidden_ref[...].astype(jnp.float32)
    for copy in later:
        copy.wait()


def project_kernel(shape, offsets, att_ref, partial_ref, gain_ref, *refs):
    count = len(offsets)
    pieces = refs[:count]
    residual_ref, normed_ref, weight, sems = refs[count:]
    rows, width = partial_ref.shape
    copies = []
    for i in range(count):
        piece_rows = pieces[i].shape[0]
        start = pl.multiple_of(offsets[i](own_place(shape)), LANES)
        copy = pltpu.make_async_copy(pieces[i], weight.at[pl.ds(start, piece_rows)], sems.at[i])
        copy.start()
        copies.append(copy)
    for copy in copies:
        copy.wait()
    step = 512
    squares = jnp.zeros((rows, 1), jnp.float32)
    for n in range(0, width, step):
        cols = slice(n, n + step)
        projected = jnp.dot(att_ref[...], weight[:, cols], preferred_element_type=jnp.float32)
        part = partial_ref[:, cols] + projected
        residual_ref[:, cols] = part
        squares = squares + lane_sum(part * part)
    factor = lax.rsqrt(squares / width + norm_eps)
    normed_ref[...] = (residual_ref[...] * factor * gain_ref[...]).astype(jnp.bfloat16)


def expert_kernel(items, shape, aux_ref, *refs):
    nz, ny, nc = shape
    count = len(items)
    sources = refs[:count]
    weights = refs[count : count + 6]
    outs = refs[count + 6 : 2 * count + 6]
    x, aux, inner, gates, ups, down, x_sems, aux_sems, w_sems = refs[2 * count + 6 :]
    member, z, y, c, _ = own_place(shape)
    rows = outs[0].shape[0]
    width, hidden = weights[0].shape
    waits = []
    for i, (kz, ky) in enumerate(items):
        block = pl.ds(i * rows, rows)
        shard = ((z ^ kz) * ny + (y ^ ky)) * nc + c
        start = pl.multiple_of(shard * rows, rows)
        extra_rows = aux_ref.at[pl.ds(start, rows)]
        waits.append(pltpu.make_async_copy(sources[i], x.at[block], x_sems.at[i]))
        waits.append(pltpu.make_async_copy(extra_rows, aux.at[block], aux_sems.at[i]))
    targets = []
    for e in range(2):
        targets += [gates.at[e], ups.at[e]]
    targets += [down.at[pl.ds(0, hidden)], down.at[pl.ds(hidden, hidden)]]
    loads = [
        pltpu.make_async_copy(weights[i], targets[i], w_sems.at[i]) for i in range(len(targets))
    ]
    for copy in loads[:2] + waits + loads[2:]:
        copy.start()
    for wait in waits:
        wait.wait()
    extra = aux[...].astype(jnp.float32)
    lane = lax.broadcasted_iota(jnp.int32, extra.shape, 1)
    is_high = (lane >= HIGH_LANE) & (lane < HIGH_LANE + TOP)
    named = pltpu.roll(extra, HIGH_LANE - ROUTE_LANE, 1)
    share = extra + pltpu.roll(extra, LANES - (LOW_LANE - HIGH_LANE), 1)
    for e in range(2):
        expert = (member ^ e).astype(jnp.float32)
        chosen = lane_sum(jnp.where(is_high & (named == expert), share, 0.0))
        loads[2 * e].wait()
        gate = jnp.dot(x[...], gates[e], preferred_element_type=jnp.float32)
        loads[2 * e + 1].wait()
        up = jnp.dot(x[...], ups[e], preferred_element_type=jnp.float32)
        inner[:, e * hidden : (e + 1) * hidden] = (
            gate * jax.nn.sigmoid(gate) * up * chosen
        ).astype(jnp.bfloat16)
    loads[4].wait()
    loads[5].wait()
    step = 512
    for n in range(0, width, step):
        result = jnp.dot(inner[...], down[:, n : n + step], preferred_element_type=jnp.float32)
        for i in range(len(items)):
            outs[i][:, n : n + step] = result[i * rows : (i + 1) * rows].astype(jnp.bfloat16)


def body(
    dims,
    hidden_in,
    queries,
    keys_values,
    segment_ids,
    routes,
    gate_weights,
    page_table,
    out_weight,
    norm_gain,
    expert_gate,
    expert_up,
    expert_down,
):
    n_dp, nz, ny, nc = dims
    shape = (nz, ny, nc)
    members = nz * ny * nc
    tok_rows, width = hidden_in.shape
    member = lax.axis_index("expert")
    z, y, c = member // (ny * nc), member // nc % ny, member % nc
    params = pltpu.CompilerParams(vmem_limit_bytes=VMEM_LIMIT)

    def at(zz, yy, cc):
        return (zz * ny + yy) * nc + cc

    places = [(a, b, d) for a in range(nz) for b in range(ny) for d in range(nc)]

    def flip(array, kz, ky, kc):
        pairs = [(at(a, b, d), at(a ^ kz, b ^ ky, d ^ kc)) for a, b, d in places]
        return lax.ppermute(array, "expert", pairs)

    def move(array, hops):
        pairs = [(at(a, b, d), at(hops[a], b, d)) for a, b, d in places if a in hops]
        return lax.ppermute(array, "expert", pairs)

    def tie(first, *others):
        return lax.optimization_barrier((first, *others))

    slot_count = tok_rows // PAGE

    kv_cols = keys_values.shape[1]
    seg_row = segment_ids.reshape(1, tok_rows)
    packed = pl.pallas_call(
        pack_kernel,
        out_shape=jax.ShapeDtypeStruct((tok_rows, kv_cols + LANES), jnp.bfloat16),
        in_specs=[vmem_spec] * 4,
        out_specs=vmem_spec,
    )(keys_values, seg_row, routes.T, gate_weights.T)
    half = out_weight.shape[0]
    split_weight = n_dp == 2 and ny == 2 and nz == 4 and half % (8 * LANES) == 0
    got = []
    if split_weight:
        quarter = half // 4
        part = quarter // nc
        first = (y ^ (z & 1)) * 2 * quarter + c * part
        for start in (first, first + quarter):
            rows = lax.dynamic_slice_in_dim(out_weight, start, part, 0)
            got.append(lax.ppermute(rows, "dp", [(0, 1), (1, 0)]))
    along = [packed] + [flip(packed, kz, 0, 0) for kz in range(1, nz)]
    beside = [packed] + [flip(packed, 0, ky, 0) for ky in range(1, ny)]

    turned = pl.pallas_call(
        turn_kernel,
        out_shape=jax.ShapeDtypeStruct((HD, HQ * tok_rows), jnp.bfloat16),
        in_specs=[vmem_spec],
        out_specs=vmem_spec,
    )(queries)
    along, beside, turned, got[:1] = tie(along, beside, turned, got[:1])
    shards = {(kz, 0, 0): along[kz] for kz in range(nz)}
    shards.update({(0, ky, 0): beside[ky] for ky in range(1, ny)})
    for kz, ky, _ in list(shards):
        shards[kz, ky, 1] = flip(shards[kz, ky, 0], 0, 0, 1)
    crossed = [(kz, ky, 0) for kz in range(1, nz) for ky in range(1, ny)]
    for kz, ky, _ in crossed:
        shards[kz, ky, 0] = flip(along[kz], 0, ky, 0)
    shards, got = tie(shards, got)
    for kz, ky, _ in crossed:
        shards[kz, ky, 1] = flip(shards[kz, ky, 0], 0, 0, 1)
    shard_list, got = tie([shards[place] for place in places], got)
    if split_weight:
        sent = [flip(got[0], 0, 1, 0), flip(got[1], 1, 0, 0)]
    own = [expert_gate[0], expert_up[0], expert_down[0]]
    own, shard_list = tie(own, shard_list)
    other = [flip(array, 0, 0, 1) for array in own]

    rest = half if split_weight else HQ * HD
    attended, partial, cache_pages, aux = pl.pallas_call(
        functools.partial(attend_kernel, shape, split_weight),
        out_shape=(
            jax.ShapeDtypeStruct((tok_rows, rest), jnp.bfloat16),
            jax.ShapeDtypeStruct((tok_rows, width), jnp.float32),
            jax.ShapeDtypeStruct((slot_count, PAGE, kv_cols), jnp.bfloat16),
            jax.ShapeDtypeStruct((members * tok_rows, LANES), jnp.bfloat16),
        ),
        in_specs=[smem_spec, vmem_spec, vmem_spec, vmem_spec] + [any_spec] * (1 + members),
        out_specs=(vmem_spec, vmem_spec, any_spec, any_spec),
        scratch_shapes=[
            pltpu.VMEM((members * tok_rows, kv_cols + LANES), jnp.bfloat16),
            pltpu.VMEM((1, HQ * tok_rows), jnp.float32),
            pltpu.VMEM((1, HQ * tok_rows), jnp.float32),
            pltpu.VMEM((HD, HQ * tok_rows), jnp.float32),
            pltpu.VMEM((tok_rows, HQ * HD), jnp.bfloat16),
            pltpu.VMEM(out_weight.shape, jnp.bfloat16),
            pltpu.SMEM((slot_count,), jnp.int32),
            pltpu.SemaphoreType.DMA((members,)),
            pltpu.SemaphoreType.DMA((2 + slot_count,)),
        ],
        compiler_params=params,
        cost_estimate=pl.CostEstimate(
            flops=ATT_FLOPS, bytes_accessed=10**6, transcendentals=0
        ),
    )(page_table, seg_row, turned, hidden_in, out_weight, *shard_list)

    if split_weight:

        def from_other(turn, index, kc):
            def offset(pos):
                pair = pos[2] ^ (pos[1] & 1) ^ turn
                return (2 * pair + index) * quarter + (pos[3] ^ kc) * part

            return offset

        attended, sent, got, other = tie(attended, sent, got, other)
        got += sent
        pieces = got + [flip(array, 0, 0, 1) for array in got]
        offsets = [
            from_other(turn, index, kc) for kc in (0, 1) for turn in (0, 1) for index in (0, 1)
        ]
    else:
        pieces = [lax.all_gather(out_weight, "dp", axis=0, tiled=True)]
        offsets = [lambda pos: 0]
    residual, normed = pl.pallas_call(
        functools.partial(project_kernel, shape, offsets),
        out_shape=(
            jax.ShapeDtypeStruct((tok_rows, width), jnp.float32),
            jax.ShapeDtypeStruct((tok_rows, width), jnp.bfloat16),
        ),
        in_specs=[vmem_spec, vmem_spec, vmem_spec] + [any_spec] * len(pieces),
        out_specs=(vmem_spec, vmem_spec),
        scratch_shapes=[
            pltpu.VMEM((rest, width), jnp.bfloat16),
            pltpu.SemaphoreType.DMA((len(pieces),)),
        ],
        compiler_params=params,
    )(attended, partial, norm_gain.reshape(1, width), *pieces)

    hidden = expert_gate.shape[2]
    results = {}
    blocks = {}

    def cross(k):
        for ky in range(1, ny):
            blocks[k, ky] = flip(blocks[k, 0], 0, ky, 0)

    def run_experts(items):
        rows = len(items) * tok_rows
        outs = pl.pallas_call(
            functools.partial(expert_kernel, items, shape),
            out_shape=[jax.ShapeDtypeStruct((tok_rows, width), jnp.bfloat16)] * len(items),
            in_specs=[any_spec] * (len(items) + 7),
            out_specs=[vmem_spec] * len(items),
            scratch_shapes=[
                pltpu.VMEM((rows, width), jnp.bfloat16),
                pltpu.VMEM((rows, LANES), jnp.bfloat16),
                pltpu.VMEM((rows, 2 * hidden), jnp.bfloat16),
                pltpu.VMEM((2, width, hidden), jnp.bfloat16),
                pltpu.VMEM((2, width, hidden), jnp.bfloat16),
                pltpu.VMEM((2 * hidden, width), jnp.bfloat16),
                pltpu.SemaphoreType.DMA((len(items),)),
                pltpu.SemaphoreType.DMA((len(items),)),
                pltpu.SemaphoreType.DMA((6,)),
            ],
            compiler_params=params,
            cost_estimate=pl.CostEstimate(
                flops=FFN_FLOPS,
                bytes_accessed=FFN_FLOPS,
                transcendentals=0,
            ),
        )(aux, *[blocks[item] for item in items], *experts)
        results.update(zip(items, outs))

    experts = [own[0], own[1], other[0], other[1], own[2], other[2]]
    blocks[0, 0] = normed
    relay = nz == 4
    across = [(0, ky) for ky in range(1, ny)]
    if not relay:
        for k in range(1, nz):
            blocks[k, 0] = flip(normed, k, 0, 0)
    else:
        blocks[1, 0] = flip(normed, 1, 0, 0)
        middle = move(normed, {1: 2, 2: 1})
    inner = (z == 1) | (z == 2)
    for k in range(nz):
        moved = []
        if relay and k == 0:
            moved = [blocks[1, 0], middle]
        elif relay and k == 1:
            moved = [move(blocks[1, 0], {1: 2, 2: 1}), move(middle, {1: 0, 2: 3})]
        elif relay and k == 2:
            moved = [move(through, {1: 0, 2: 3})]
        elif not relay and k + 1 < nz:
            moved = [blocks[k + 1, 0]]
        cross(k)
        across = [(k, ky) for ky in range(1, ny)]
        arrived, moved = tie([blocks[item] for item in across], moved)
        blocks.update(zip(across, arrived))
        if not relay and k + 1 < nz:
            blocks[k + 1, 0] = moved[0]
        elif k == 0:
            blocks[1, 0], middle = moved
        elif k == 1:
            through = moved[0]
            blocks[2, 0] = jnp.where(inner, through, moved[1])
        elif k == 2:
            blocks[3, 0] = jnp.where(inner, middle, moved[0])
        if k == nz - 2:
            late = [(k, ky) for ky in range(ny)] + [(k + 1, 0)]
            run_experts(late)
    across = [(nz - 1, ky) for ky in range(1, ny)]
    arrived, finished = tie(
        [blocks[item] for item in across], [results[item] for item in late]
    )
    blocks.update(zip(across, arrived))
    results.update(zip(late, finished))
    run_experts(across)
    early = [(k, ky) for k in range(nz - 2) for ky in range(ny)]
    blocks[0, 0], results[nz - 1, ny - 1] = tie(blocks[0, 0], results[nz - 1, ny - 1])
    run_experts(early)

    def as_float(array):
        return array.astype(jnp.float32)

    def back(k):
        return [flip(results[k, ky], 0, ky, 0) for ky in range(1, ny)]

    def total(k, arrived):
        value = as_float(results[k, 0])
        for array in arrived:
            value = value + as_float(array)
        return value

    def small(array):
        return array.astype(jnp.bfloat16)

    if relay:
        out, into, middles = {0: 1, 3: 2}, {1: 0, 2: 3}, {1: 2, 2: 1}
        back3, finished = tie(back(3), [results[item] for item in early])
        results.update(zip(early, finished))
        third = total(3, back3)
        far, back2 = tie(move(small(third), out), back(2))
        second = total(2, back2)
        near = move(small(second), out)
        far = move(small(second + as_float(far)), middles)
        far, near, back1 = tie(far, near, back(1))
        first = total(1, back1) + as_float(far)
        near = move(small(third + as_float(near)), middles)
        far = flip(small(first), 1, 0, 0)
        combined = total(0, back(0)) + as_float(far) + as_float(near)
    else:
        combined = total(0, back(0))
        for k in range(nz - 1, 0, -1):
            combined = combined + as_float(flip(small(total(k, back(k))), k, 0, 0))
    hidden_out = (residual + combined).astype(jnp.bfloat16)
    return (hidden_out, cache_pages)


def split_axis(mesh):
    n_dp = mesh.shape["dp"]
    members = mesh.shape["expert"]
    nc = 2
    ny = n_dp if members % (nc * n_dp) == 0 else 1
    return (n_dp, members // (nc * ny), ny, nc)


def solution(mesh):
    return jax.shard_map(
        functools.partial(body, split_axis(mesh)),
        mesh=mesh,
        in_specs=(
            P(("dp", "expert"), None),
            P(("dp", "expert"), None),
            P(("dp", "expert"), None),
            P("dp", "expert"),
            P(("dp", "expert"), None),
            P(("dp", "expert"), None),
            P("dp", None),
            P("dp", None),
            P(),
            P("expert", None, None),
            P("expert", None, None),
            P("expert", None, None),
        ),
        out_specs=(P(("dp", "expert"), None), P(("dp", "expert"), None, None)),
        check_vma=False,
    )
```

```python
import functools
import math

import jax
import jax.numpy as jnp
from jax import lax
from jax.experimental import pallas as pl
from jax.experimental.pallas import tpu as pltpu
from jax.sharding import PartitionSpec as P

HD = 128
HQ = 16
HK = 2
TOP = 8
PAGE = 16
LANES = 128
KEY_BLOCK = 256

neg_big = -1e30
norm_eps = 1e-06

ROUTE_LANE = 8
HIGH_LANE = 16
LOW_LANE = 24

VMEM_LIMIT = 60 * 1024 * 1024
CALL_BLOCKS = 4
EXPERT_COST = 10**6
ATTEND_COST = 10**6

vmem_spec = pl.BlockSpec(memory_space=pltpu.VMEM)
smem_spec = pl.BlockSpec(memory_space=pltpu.SMEM)
any_spec = pl.BlockSpec(memory_space=pltpu.HBM)


def own_place(shape):
    _, ny, nc = shape
    member = lax.axis_index("expert")
    return member, member // (ny * nc), member // nc % ny, member % nc, lax.axis_index("dp")


def lane_sum(values):
    return jnp.sum(values, axis=1, keepdims=True)


def pack_kernel(kv_ref, seg_ref, routes_ref, weights_ref, out_ref):
    rows, kv_cols = kv_ref.shape
    out_ref[:, :kv_cols] = kv_ref[...]
    row_id = lax.broadcasted_iota(jnp.int32, (rows, rows), 0)
    col_id = lax.broadcasted_iota(jnp.int32, (rows, rows), 1)
    identity = jnp.where(row_id == col_id, 1.0, 0.0).astype(jnp.bfloat16)
    weights = weights_ref[...]
    shares = weights / jnp.sum(weights, axis=0, keepdims=True)
    high = shares.astype(jnp.bfloat16).astype(jnp.float32)
    seg = jnp.broadcast_to(seg_ref[...].astype(jnp.float32), (ROUTE_LANE, rows))
    lines = [seg, routes_ref[...].astype(jnp.float32), high, shares - high]
    lines.append(jnp.zeros((LANES - LOW_LANE - TOP, rows), jnp.float32))
    lines = jnp.concatenate(lines, axis=0).astype(jnp.bfloat16)
    turned = lax.dot_general(
        identity, lines, (((1,), (1,)), ((), ())), preferred_element_type=jnp.float32
    )
    out_ref[:, kv_cols:] = turned.astype(jnp.bfloat16)


def turn_kernel(q_ref, out_ref):
    rows = q_ref.shape[0]
    for h in range(HQ):
        part = q_ref[:, h * HD : (h + 1) * HD].astype(jnp.float32)
        out_ref[:, h * rows : (h + 1) * rows] = part.T.astype(jnp.bfloat16)


def attend_kernel(shape, own_part, table_ref, seg_ref, q_ref, hidden_ref, weight_ref, *refs):
    nz, ny, nc = shape
    count = nz * ny * nc
    shards = refs[:count]
    out_ref, partial_ref, cache_ref, aux_ref = refs[count : count + 4]
    held, top, total, acc, attended, weight, pages, sems, more_sems = refs[count + 4 :]
    tok_rows, width = hidden_ref.shape
    kv_width = HK * HD
    member, z, y, c, side = own_place(shape)
    copies = []
    for i in range(count):
        kz, ky, kc = i // (ny * nc), i // nc % ny, i % nc
        shard = ((z ^ kz) * ny + (y ^ ky)) * nc + (c ^ kc)
        start = pl.multiple_of(shard * tok_rows, tok_rows)
        copy = pltpu.make_async_copy(shards[i], held.at[pl.ds(start, tok_rows)], sems.at[i])
        copy.start()
        copies.append(copy)
    weight_copy = pltpu.make_async_copy(weight_ref, weight, more_sems.at[0])
    if own_part:
        weight_copy.start()
    top[...] = jnp.full(top.shape, neg_big, jnp.float32)
    total[...] = jnp.zeros(total.shape, jnp.float32)
    acc[...] = jnp.zeros(acc.shape, jnp.float32)
    slots = cache_ref.shape[0]

    def find_slot(page, carried):
        slot = table_ref[0, page] - member * slots

        @pl.when((slot >= 0) & (slot < slots))
        def _():
            pages[slot] = page

        return carried

    lax.fori_loop(0, table_ref.shape[1], find_slot, 0, unroll=8)
    for copy in copies:
        copy.wait()
    later = [pltpu.make_async_copy(held.at[:, 2 * kv_width :], aux_ref, more_sems.at[1])]
    for s in range(slots):
        start = pl.multiple_of(pages[s] * PAGE, PAGE)
        page = held.at[pl.ds(start, PAGE), pl.ds(0, 2 * kv_width)]
        later.append(pltpu.make_async_copy(page, cache_ref.at[s], more_sems.at[2 + s]))
    for copy in later:
        copy.start()
    own_seg = seg_ref[...].astype(jnp.float32)

    def count_lower(s, below):
        start = pl.multiple_of(s * tok_rows, tok_rows)
        seg = held[pl.ds(start, tok_rows), 2 * kv_width :][:, 0:1].astype(jnp.float32)
        return below + jnp.where(seg < own_seg, 1.0, 0.0)

    below = lax.fori_loop(0, member + 1, count_lower, jnp.zeros((tok_rows, tok_rows), jnp.float32))
    seg_start = jnp.sum(below, axis=0, keepdims=True).astype(jnp.int32)
    first_row = member * tok_rows
    query_pos = first_row + lax.broadcasted_iota(jnp.int32, (1, tok_rows), 1)
    last_block = first_row // KEY_BLOCK
    first_block = jnp.min(seg_start) // KEY_BLOCK
    scale = 1.0 / math.sqrt(HD)
    heads = 4
    cols = heads * tok_rows
    groups = HQ // HK

    def attend(step, carried):
        base = pl.multiple_of((last_block - step) * KEY_BLOCK, KEY_BLOCK)
        key_pos = base + lax.broadcasted_iota(jnp.int32, (KEY_BLOCK, tok_rows), 0)
        seen = (key_pos >= seg_start) & (key_pos <= query_pos)
        bias = jnp.where(seen, 0.0, neg_big)
        bias = jnp.concatenate([bias] * heads, axis=1)
        for g in range(HK):
            key = held[pl.ds(base, KEY_BLOCK), g * HD : (g + 1) * HD]
            value = held[pl.ds(base, KEY_BLOCK), kv_width + g * HD : kv_width + (g + 1) * HD]
            for u in range(0, groups, heads):
                unit = slice((g * groups + u) * tok_rows, (g * groups + u) * tok_rows + cols)
                scores = jnp.dot(key, q_ref[:, unit], preferred_element_type=jnp.float32) + bias
                old_top = top[:, unit]
                new_top = jnp.maximum(old_top, jnp.max(scores, axis=0, keepdims=True))
                weights = jnp.exp((scores - new_top) * scale)
                factor = jnp.exp((old_top - new_top) * scale)
                top[:, unit] = new_top
                total[:, unit] = total[:, unit] * factor + jnp.sum(weights, axis=0, keepdims=True)
                added = lax.dot_general(
                    value,
                    weights.astype(jnp.bfloat16),
                    (((0,), (0,)), ((), ())),
                    preferred_element_type=jnp.float32,
                )
                acc[:, unit] = acc[:, unit] * factor + added
        return carried

    lax.fori_loop(0, last_block - first_block + 1, attend, 0)
    for h in range(HQ):
        unit = slice(h * tok_rows, (h + 1) * tok_rows)
        head = acc[:, unit] / total[:, unit]
        attended[:, h * HD : (h + 1) * HD] = head.T.astype(jnp.bfloat16)
    step = 512
    if own_part:
        half = weight.shape[0]
        mine = attended[:, pl.ds(pl.multiple_of(side * half, half), half)]
        out_ref[...] = attended[:, pl.ds(pl.multiple_of((1 - side) * half, half), half)]
        weight_copy.wait()
        for n in range(0, width, step):
            part = slice(n, n + step)
            partial_ref[:, part] = hidden_ref[:, part].astype(jnp.float32) + jnp.dot(
                mine, weight[:, part], preferred_element_type=jnp.float32
            )
    else:
        out_ref[...] = attended[...]
        partial_ref[...] = hidden_ref[...].astype(jnp.float32)
    for copy in later:
        copy.wait()


def project_kernel(shape, offsets, att_ref, partial_ref, gain_ref, *refs):
    count = len(offsets)
    pieces = refs[:count]
    residual_ref, normed_ref, weight, sems = refs[count:]
    rows, width = partial_ref.shape
    copies = []
    for i in range(count):
        piece_rows = pieces[i].shape[0]
        start = pl.multiple_of(offsets[i](own_place(shape)), LANES)
        copy = pltpu.make_async_copy(pieces[i], weight.at[pl.ds(start, piece_rows)], sems.at[i])
        copy.start()
        copies.append(copy)
    for copy in copies:
        copy.wait()
    step = 512
    squares = jnp.zeros((rows, 1), jnp.float32)
    for n in range(0, width, step):
        cols = slice(n, n + step)
        projected = jnp.dot(att_ref[...], weight[:, cols], preferred_element_type=jnp.float32)
        part = partial_ref[:, cols] + projected
        residual_ref[:, cols] = part
        squares = squares + lane_sum(part * part)
    factor = lax.rsqrt(squares / width + norm_eps)
    normed_ref[...] = (residual_ref[...] * factor * gain_ref[...]).astype(jnp.bfloat16)


def expert_kernel(items, shape, aux_ref, *refs):
    nz, ny, nc = shape
    count = len(items)
    sources = refs[:count]
    weights = refs[count : count + 6]
    outs = refs[count + 6 : 2 * count + 6]
    x, aux, inner, gates, ups, down, x_sems, aux_sems, w_sems = refs[2 * count + 6 :]
    member, z, y, c, _ = own_place(shape)
    rows = outs[0].shape[0]
    width, hidden = weights[0].shape
    waits = []
    for i, (kz, ky) in enumerate(items):
        block = pl.ds(i * rows, rows)
        shard = ((z ^ kz) * ny + (y ^ ky)) * nc + c
        start = pl.multiple_of(shard * rows, rows)
        extra_rows = aux_ref.at[pl.ds(start, rows)]
        waits.append(pltpu.make_async_copy(sources[i], x.at[block], x_sems.at[i]))
        waits.append(pltpu.make_async_copy(extra_rows, aux.at[block], aux_sems.at[i]))
    targets = []
    for e in range(2):
        targets += [gates.at[e], ups.at[e]]
    targets += [down.at[pl.ds(0, hidden)], down.at[pl.ds(hidden, hidden)]]
    loads = [
        pltpu.make_async_copy(weights[i], targets[i], w_sems.at[i]) for i in range(len(targets))
    ]
    for copy in loads[:2] + waits + loads[2:]:
        copy.start()
    for wait in waits:
        wait.wait()
    extra = aux[...].astype(jnp.float32)
    lane = lax.broadcasted_iota(jnp.int32, extra.shape, 1)
    is_high = (lane >= HIGH_LANE) & (lane < HIGH_LANE + TOP)
    named = pltpu.roll(extra, HIGH_LANE - ROUTE_LANE, 1)
    share = extra + pltpu.roll(extra, LANES - (LOW_LANE - HIGH_LANE), 1)
    for e in range(2):
        expert = (member ^ e).astype(jnp.float32)
        chosen = lane_sum(jnp.where(is_high & (named == expert), share, 0.0))
        loads[2 * e].wait()
        gate = jnp.dot(x[...], gates[e], preferred_element_type=jnp.float32)
        loads[2 * e + 1].wait()
        up = jnp.dot(x[...], ups[e], preferred_element_type=jnp.float32)
        inner[:, e * hidden : (e + 1) * hidden] = (
            gate * jax.nn.sigmoid(gate) * up * chosen
        ).astype(jnp.bfloat16)
    loads[4].wait()
    loads[5].wait()
    step = 512
    for n in range(0, width, step):
        result = jnp.dot(inner[...], down[:, n : n + step], preferred_element_type=jnp.float32)
        for i in range(len(items)):
            outs[i][:, n : n + step] = result[i * rows : (i + 1) * rows].astype(jnp.bfloat16)


def body(
    dims,
    hidden_in,
    queries,
    keys_values,
    segment_ids,
    routes,
    gate_weights,
    page_table,
    out_weight,
    norm_gain,
    expert_gate,
    expert_up,
    expert_down,
):
    n_dp, nz, ny, nc = dims
    shape = (nz, ny, nc)
    members = nz * ny * nc
    tok_rows, width = hidden_in.shape
    member = lax.axis_index("expert")
    z, y, c = member // (ny * nc), member // nc % ny, member % nc
    params = pltpu.CompilerParams(vmem_limit_bytes=VMEM_LIMIT)

    def at(zz, yy, cc):
        return (zz * ny + yy) * nc + cc

    places = [(a, b, d) for a in range(nz) for b in range(ny) for d in range(nc)]

    def flip(array, kz, ky, kc):
        pairs = [(at(a, b, d), at(a ^ kz, b ^ ky, d ^ kc)) for a, b, d in places]
        return lax.ppermute(array, "expert", pairs)

    def move(array, hops):
        pairs = [(at(a, b, d), at(hops[a], b, d)) for a, b, d in places if a in hops]
        return lax.ppermute(array, "expert", pairs)

    def tie(first, *others):
        return lax.optimization_barrier((first, *others))

    slot_count = tok_rows // PAGE

    kv_cols = keys_values.shape[1]
    seg_row = segment_ids.reshape(1, tok_rows)
    packed = pl.pallas_call(
        pack_kernel,
        out_shape=jax.ShapeDtypeStruct((tok_rows, kv_cols + LANES), jnp.bfloat16),
        in_specs=[vmem_spec] * 4,
        out_specs=vmem_spec,
    )(keys_values, seg_row, routes.T, gate_weights.T)
    half = out_weight.shape[0]
    split_weight = n_dp == 2 and ny == 2 and nz == 4 and half % (8 * LANES) == 0
    got = []
    if split_weight:
        quarter = half // 4
        part = quarter // nc
        first = (y ^ (z & 1)) * 2 * quarter + c * part
        held_back, packed = tie(out_weight, packed)
        starts = (first, first + quarter)
        got = [lax.dynamic_slice_in_dim(held_back, start, part, 0) for start in starts]
        got[0] = lax.ppermute(got[0], "dp", [(0, 1), (1, 0)])
    along = [packed] + [flip(packed, kz, 0, 0) for kz in range(1, nz)]
    beside = [packed] + [flip(packed, 0, ky, 0) for ky in range(1, ny)]

    turned = pl.pallas_call(
        turn_kernel,
        out_shape=jax.ShapeDtypeStruct((HD, HQ * tok_rows), jnp.bfloat16),
        in_specs=[vmem_spec],
        out_specs=vmem_spec,
    )(queries)
    along, beside, turned, got = tie(along, beside, turned, got)
    if split_weight:
        got[1] = lax.ppermute(got[1], "dp", [(0, 1), (1, 0)])
    shards = {(kz, 0, 0): along[kz] for kz in range(nz)}
    shards.update({(0, ky, 0): beside[ky] for ky in range(1, ny)})
    near = list(shards)
    crossed = [(kz, ky, 0) for kz in range(1, nz) for ky in range(1, ny)]
    for kz, ky, _ in crossed:
        shards[kz, ky, 0] = flip(along[kz], 0, ky, 0)
    arrays, shards[crossed[0]] = tie([shards[name] for name in near], shards[crossed[0]])
    shards.update(zip(near, arrays))
    for kz, ky, _ in near:
        shards[kz, ky, 1] = flip(shards[kz, ky, 0], 0, 0, 1)
    shards = tie(shards)[0]
    for kz, ky, _ in crossed:
        shards[kz, ky, 1] = flip(shards[kz, ky, 0], 0, 0, 1)
    shard_list, got = tie([shards[place] for place in places], got)
    if split_weight:
        sent = [flip(got[0], 0, 1, 0), flip(got[1], 1, 0, 0)]
        got += [flip(array, 0, 0, 1) for array in got]
    own = [expert_gate[0], expert_up[0], expert_down[0]]
    own, shard_list = tie(own, shard_list)
    other = [flip(own[2], 0, 0, 1)]

    rest = half if split_weight else HQ * HD
    attended, partial, cache_pages, aux = pl.pallas_call(
        functools.partial(attend_kernel, shape, split_weight),
        out_shape=(
            jax.ShapeDtypeStruct((tok_rows, rest), jnp.bfloat16),
            jax.ShapeDtypeStruct((tok_rows, width), jnp.float32),
            jax.ShapeDtypeStruct((slot_count, PAGE, kv_cols), jnp.bfloat16),
            jax.ShapeDtypeStruct((members * tok_rows, LANES), jnp.bfloat16),
        ),
        in_specs=[smem_spec, vmem_spec, vmem_spec, vmem_spec] + [any_spec] * (1 + members),
        out_specs=(vmem_spec, vmem_spec, any_spec, any_spec),
        scratch_shapes=[
            pltpu.VMEM((members * tok_rows, kv_cols + LANES), jnp.bfloat16),
            pltpu.VMEM((1, HQ * tok_rows), jnp.float32),
            pltpu.VMEM((1, HQ * tok_rows), jnp.float32),
            pltpu.VMEM((HD, HQ * tok_rows), jnp.float32),
            pltpu.VMEM((tok_rows, HQ * HD), jnp.bfloat16),
            pltpu.VMEM(out_weight.shape, jnp.bfloat16),
            pltpu.SMEM((slot_count,), jnp.int32),
            pltpu.SemaphoreType.DMA((members,)),
            pltpu.SemaphoreType.DMA((2 + slot_count,)),
        ],
        compiler_params=params,
        cost_estimate=pl.CostEstimate(
            flops=ATTEND_COST, bytes_accessed=10**6, transcendentals=0
        ),
    )(page_table, seg_row, turned, hidden_in, out_weight, *shard_list)

    if split_weight:

        def from_other(turn, index, kc):
            def offset(pos):
                pair = pos[2] ^ (pos[1] & 1) ^ turn
                return (2 * pair + index) * quarter + (pos[3] ^ kc) * part

            return offset

        attended, sent, other = tie(attended, sent, other)
        pieces = got + sent + [flip(array, 0, 0, 1) for array in sent]
        offsets = [
            from_other(turn, index, kc) for turn in (0, 1) for kc in (0, 1) for index in (0, 1)
        ]
    else:
        pieces = [lax.all_gather(out_weight, "dp", axis=0, tiled=True)]
        offsets = [lambda pos: 0]
    residual, normed = pl.pallas_call(
        functools.partial(project_kernel, shape, offsets),
        out_shape=(
            jax.ShapeDtypeStruct((tok_rows, width), jnp.float32),
            jax.ShapeDtypeStruct((tok_rows, width), jnp.bfloat16),
        ),
        in_specs=[vmem_spec, vmem_spec, vmem_spec] + [any_spec] * len(pieces),
        out_specs=(vmem_spec, vmem_spec),
        scratch_shapes=[
            pltpu.VMEM((rest, width), jnp.bfloat16),
            pltpu.SemaphoreType.DMA((len(pieces),)),
        ],
        compiler_params=pltpu.CompilerParams(vmem_limit_bytes=20 * 1024 * 1024),
    )(attended, partial, norm_gain.reshape(1, width), *pieces)

    hidden = expert_gate.shape[2]
    results = {}
    blocks = {}

    def cross(k):
        for ky in range(1, ny):
            blocks[k, ky] = flip(blocks[k, 0], 0, ky, 0)

    def run_experts(items):
        for start in range(0, len(items), CALL_BLOCKS):
            run_call(items[start : start + CALL_BLOCKS])

    def run_call(items):
        rows = len(items) * tok_rows
        outs = pl.pallas_call(
            functools.partial(expert_kernel, items, shape),
            out_shape=[jax.ShapeDtypeStruct((tok_rows, width), jnp.bfloat16)] * len(items),
            in_specs=[any_spec] * (len(items) + 7),
            out_specs=[vmem_spec] * len(items),
            scratch_shapes=[
                pltpu.VMEM((rows, width), jnp.bfloat16),
                pltpu.VMEM((rows, LANES), jnp.bfloat16),
                pltpu.VMEM((rows, 2 * hidden), jnp.bfloat16),
                pltpu.VMEM((2, width, hidden), jnp.bfloat16),
                pltpu.VMEM((2, width, hidden), jnp.bfloat16),
                pltpu.VMEM((2 * hidden, width), jnp.bfloat16),
                pltpu.SemaphoreType.DMA((len(items),)),
                pltpu.SemaphoreType.DMA((len(items),)),
                pltpu.SemaphoreType.DMA((6,)),
            ],
            compiler_params=pltpu.CompilerParams(vmem_limit_bytes=24 * 1024 * 1024),
            cost_estimate=pl.CostEstimate(
                flops=EXPERT_COST,
                bytes_accessed=EXPERT_COST,
                transcendentals=0,
            ),
        )(aux, *[blocks[item] for item in items], *experts)
        results.update(zip(items, outs))

    own[:2], normed = tie(own[:2], normed)
    other = [flip(array, 0, 0, 1) for array in own[:2]] + other
    experts = [own[0], own[1], other[0], other[1], own[2], other[2]]
    blocks[0, 0] = normed
    relay = nz == 4
    inner = (z == 1) | (z == 2)
    hops = {}
    if relay:
        out, into, middles = {0: 1, 3: 2}, {1: 0, 2: 3}, {1: 2, 2: 1}
        hops[1] = flip(normed, 1, 0, 0)
        middle = move(normed, middles)
    for k in range(nz):
        if not relay and k > 0:
            blocks[k, 0] = flip(normed, k, 0, 0)
        elif k == 1:
            blocks[1, 0] = hops[1]
        elif k == 2:
            ends = move(middle, into)
            hops[2] = move(blocks[1, 0], middles)
            blocks[2, 0] = jnp.where(inner, hops[2], ends)
        elif k == 3:
            blocks[3, 0] = jnp.where(inner, middle, move(hops[2], into))
        if k > 0:
            before = [(k - 1, ky) for ky in range(1, ny)]
            blocks[k, 0], arrived = tie(blocks[k, 0], [blocks[item] for item in before])
            blocks.update(zip(before, arrived))
        cross(k)
        if k == nz - 2:
            late = [(k, ky) for ky in range(ny)] + [(k + 1, 0)]
    run_experts(late)
    across = [(nz - 1, ky) for ky in range(1, ny)]
    arrived, finished = tie(
        [blocks[item] for item in across], [results[item] for item in late]
    )
    blocks.update(zip(across, arrived))
    results.update(zip(late, finished))
    run_experts(across)
    early = [(k, ky) for k in range(nz - 2) for ky in range(ny)]
    blocks[0, 0], results[nz - 1, ny - 1] = tie(blocks[0, 0], results[nz - 1, ny - 1])
    run_experts(early)

    def as_float(array):
        return array.astype(jnp.float32)

    def back(k):
        return [flip(results[k, ky], 0, ky, 0) for ky in range(1, ny)]

    def total(k, arrived):
        value = as_float(results[k, 0])
        for array in arrived:
            value = value + as_float(array)
        return value

    def small(array):
        return array.astype(jnp.bfloat16)

    if relay:

        def next_back(k, arrived):
            items = [(k, ky) for ky in range(1, ny)]
            tied, arrived = tie([results[item] for item in items], arrived)
            results.update(zip(items, tied))
            return arrived, back(k)

        back3, finished = tie(back(3), [results[item] for item in early])
        results.update(zip(early, finished))
        back3, back2 = next_back(2, back3)
        third = total(3, back3)
        far = move(small(third), out)
        back2, back1 = next_back(1, back2)
        second = total(2, back2)
        far = move(small(second + as_float(far)), middles)
        near = move(small(second), out)
        back1, back0 = next_back(0, back1)
        far = flip(small(total(1, back1) + as_float(far)), 1, 0, 0)
        near = move(small(third + as_float(near)), middles)
        combined = total(0, back0) + as_float(far) + as_float(near)
    else:
        combined = total(0, back(0))
        for k in range(nz - 1, 0, -1):
            combined = combined + as_float(flip(small(total(k, back(k))), k, 0, 0))
    hidden_out = (residual + combined).astype(jnp.bfloat16)
    return (hidden_out, cache_pages)


def split_axis(mesh):
    n_dp = mesh.shape["dp"]
    members = mesh.shape["expert"]
    nc = 2
    ny = n_dp if members % (nc * n_dp) == 0 else 1
    return (n_dp, members // (nc * ny), ny, nc)


def solution(mesh):
    return jax.shard_map(
        functools.partial(body, split_axis(mesh)),
        mesh=mesh,
        in_specs=(
            P(("dp", "expert"), None),
            P(("dp", "expert"), None),
            P(("dp", "expert"), None),
            P("dp", "expert"),
            P(("dp", "expert"), None),
            P(("dp", "expert"), None),
            P("dp", None),
            P("dp", None),
            P(),
            P("expert", None, None),
            P("expert", None, None),
            P("expert", None, None),
        ),
        out_specs=(P(("dp", "expert"), None), P(("dp", "expert"), None, None)),
        check_vma=False,
    )
```

```python
import functools
import math

import jax
import jax.numpy as jnp
from jax import lax
from jax.experimental import pallas as pl
from jax.experimental.pallas import tpu as pltpu
from jax.sharding import PartitionSpec as P

HD = 128
HQ = 16
HK = 2
TOP = 8
PAGE = 16
LANES = 128
KEY_BLOCK = 256

neg_big = -1e30
norm_eps = 1e-06

ROUTE_LANE = 8
HIGH_LANE = 16
LOW_LANE = 24

VMEM_LIMIT = 60 * 1024 * 1024
CALL_BLOCKS = 4
EXPERT_COST = 10**6
ATTEND_COST = 10**6

vmem_spec = pl.BlockSpec(memory_space=pltpu.VMEM)
smem_spec = pl.BlockSpec(memory_space=pltpu.SMEM)
any_spec = pl.BlockSpec(memory_space=pltpu.HBM)


def own_place(shape):
    _, ny, nc = shape
    member = lax.axis_index("expert")
    return member, member // (ny * nc), member // nc % ny, member % nc, lax.axis_index("dp")


def lane_sum(values):
    return jnp.sum(values, axis=1, keepdims=True)


def pack_kernel(kv_ref, seg_ref, routes_ref, weights_ref, out_ref):
    rows, kv_cols = kv_ref.shape
    out_ref[:, :kv_cols] = kv_ref[...]
    row_id = lax.broadcasted_iota(jnp.int32, (rows, rows), 0)
    col_id = lax.broadcasted_iota(jnp.int32, (rows, rows), 1)
    identity = jnp.where(row_id == col_id, 1.0, 0.0).astype(jnp.bfloat16)
    weights = weights_ref[...]
    shares = weights / jnp.sum(weights, axis=0, keepdims=True)
    high = shares.astype(jnp.bfloat16).astype(jnp.float32)
    seg = jnp.broadcast_to(seg_ref[...].astype(jnp.float32), (ROUTE_LANE, rows))
    lines = [seg, routes_ref[...].astype(jnp.float32), high, shares - high]
    lines.append(jnp.zeros((LANES - LOW_LANE - TOP, rows), jnp.float32))
    lines = jnp.concatenate(lines, axis=0).astype(jnp.bfloat16)
    turned = lax.dot_general(
        identity, lines, (((1,), (1,)), ((), ())), preferred_element_type=jnp.float32
    )
    out_ref[:, kv_cols:] = turned.astype(jnp.bfloat16)


def turn_kernel(q_ref, out_ref):
    rows = q_ref.shape[0]
    for h in range(HQ):
        part = q_ref[:, h * HD : (h + 1) * HD].astype(jnp.float32)
        out_ref[:, h * rows : (h + 1) * rows] = part.T.astype(jnp.bfloat16)


def attend_kernel(shape, own_part, table_ref, seg_ref, q_ref, hidden_ref, weight_ref, *refs):
    nz, ny, nc = shape
    count = nz * ny * nc
    shards = refs[:count]
    out_ref, partial_ref, cache_ref, aux_ref = refs[count : count + 4]
    held, top, total, acc, attended, weight, pages, sems, more_sems = refs[count + 4 :]
    tok_rows, width = hidden_ref.shape
    kv_width = HK * HD
    member, z, y, c, side = own_place(shape)
    copies = []
    for i in range(count):
        kz, ky, kc = i // (ny * nc), i // nc % ny, i % nc
        shard = ((z ^ kz) * ny + (y ^ ky)) * nc + (c ^ kc)
        start = pl.multiple_of(shard * tok_rows, tok_rows)
        copy = pltpu.make_async_copy(shards[i], held.at[pl.ds(start, tok_rows)], sems.at[i])
        copy.start()
        copies.append(copy)
    weight_copy = pltpu.make_async_copy(weight_ref, weight, more_sems.at[0])
    if own_part:
        weight_copy.start()
    top[...] = jnp.full(top.shape, neg_big, jnp.float32)
    total[...] = jnp.zeros(total.shape, jnp.float32)
    acc[...] = jnp.zeros(acc.shape, jnp.float32)
    slots = cache_ref.shape[0]

    def find_slot(page, carried):
        slot = table_ref[0, page] - member * slots

        @pl.when((slot >= 0) & (slot < slots))
        def _():
            pages[slot] = page

        return carried

    lax.fori_loop(0, table_ref.shape[1], find_slot, 0, unroll=8)
    for copy in copies:
        copy.wait()
    later = [pltpu.make_async_copy(held.at[:, 2 * kv_width :], aux_ref, more_sems.at[1])]
    for s in range(slots):
        start = pl.multiple_of(pages[s] * PAGE, PAGE)
        page = held.at[pl.ds(start, PAGE), pl.ds(0, 2 * kv_width)]
        later.append(pltpu.make_async_copy(page, cache_ref.at[s], more_sems.at[2 + s]))
    for copy in later:
        copy.start()
    own_seg = seg_ref[...].astype(jnp.float32)

    def count_lower(s, below):
        start = pl.multiple_of(s * tok_rows, tok_rows)
        seg = held[pl.ds(start, tok_rows), 2 * kv_width :][:, 0:1].astype(jnp.float32)
        return below + jnp.where(seg < own_seg, 1.0, 0.0)

    below = lax.fori_loop(0, member + 1, count_lower, jnp.zeros((tok_rows, tok_rows), jnp.float32))
    seg_start = jnp.sum(below, axis=0, keepdims=True).astype(jnp.int32)
    first_row = member * tok_rows
    query_pos = first_row + lax.broadcasted_iota(jnp.int32, (1, tok_rows), 1)
    last_block = first_row // KEY_BLOCK
    first_block = jnp.min(seg_start) // KEY_BLOCK
    scale = 1.0 / math.sqrt(HD)
    heads = 4
    cols = heads * tok_rows
    groups = HQ // HK

    def attend(step, carried):
        base = pl.multiple_of((last_block - step) * KEY_BLOCK, KEY_BLOCK)
        key_pos = base + lax.broadcasted_iota(jnp.int32, (KEY_BLOCK, tok_rows), 0)
        seen = (key_pos >= seg_start) & (key_pos <= query_pos)
        bias = jnp.where(seen, 0.0, neg_big)
        bias = jnp.concatenate([bias] * heads, axis=1)
        units = [
            (g, slice((g * groups + u) * tok_rows, (g * groups + u) * tok_rows + cols))
            for g in range(HK)
            for u in range(0, groups, heads)
        ]
        keys = [held[pl.ds(base, KEY_BLOCK), g * HD : (g + 1) * HD] for g in range(HK)]
        values = []
        for g in range(HK):
            value = held[pl.ds(base, KEY_BLOCK), kv_width + g * HD : kv_width + (g + 1) * HD]
            values.append(value.astype(jnp.float32).T.astype(jnp.bfloat16))
        scores = [
            jnp.dot(keys[g], q_ref[:, unit], preferred_element_type=jnp.float32) + bias
            for g, unit in units
        ]
        old_tops = [top[:, unit] for _, unit in units]
        new_tops = [
            jnp.maximum(old, jnp.max(score, axis=0, keepdims=True))
            for old, score in zip(old_tops, scores)
        ]
        weights = [jnp.exp((score - new) * scale) for score, new in zip(scores, new_tops)]
        added = [
            jnp.dot(values[g], weight.astype(jnp.bfloat16), preferred_element_type=jnp.float32)
            for (g, _), weight in zip(units, weights)
        ]
        for i, (_, unit) in enumerate(units):
            factor = jnp.exp((old_tops[i] - new_tops[i]) * scale)
            top[:, unit] = new_tops[i]
            sums = jnp.sum(weights[i], axis=0, keepdims=True)
            total[:, unit] = total[:, unit] * factor + sums
            acc[:, unit] = acc[:, unit] * factor + added[i]
        return carried

    lax.fori_loop(0, last_block - first_block + 1, attend, 0)
    for h in range(HQ):
        unit = slice(h * tok_rows, (h + 1) * tok_rows)
        head = acc[:, unit] / total[:, unit]
        attended[:, h * HD : (h + 1) * HD] = head.T.astype(jnp.bfloat16)
    step = 512
    if own_part:
        half = weight.shape[0]
        mine = attended[:, pl.ds(pl.multiple_of(side * half, half), half)]
        out_ref[...] = attended[:, pl.ds(pl.multiple_of((1 - side) * half, half), half)]
        weight_copy.wait()
        for n in range(0, width, step):
            part = slice(n, n + step)
            partial_ref[:, part] = hidden_ref[:, part].astype(jnp.float32) + jnp.dot(
                mine, weight[:, part], preferred_element_type=jnp.float32
            )
    else:
        out_ref[...] = attended[...]
        partial_ref[...] = hidden_ref[...].astype(jnp.float32)
    for copy in later:
        copy.wait()


def project_kernel(shape, offsets, att_ref, partial_ref, gain_ref, *refs):
    count = len(offsets)
    pieces = refs[:count]
    residual_ref, normed_ref, weight, sems = refs[count:]
    rows, width = partial_ref.shape
    copies = []
    for i in range(count):
        piece_rows = pieces[i].shape[0]
        start = pl.multiple_of(offsets[i](own_place(shape)), LANES)
        copy = pltpu.make_async_copy(pieces[i], weight.at[pl.ds(start, piece_rows)], sems.at[i])
        copy.start()
        copies.append(copy)
    for copy in copies:
        copy.wait()
    step = 512
    squares = jnp.zeros((rows, 1), jnp.float32)
    for n in range(0, width, step):
        cols = slice(n, n + step)
        projected = jnp.dot(att_ref[...], weight[:, cols], preferred_element_type=jnp.float32)
        part = partial_ref[:, cols] + projected
        residual_ref[:, cols] = part
        squares = squares + lane_sum(part * part)
    factor = lax.rsqrt(squares / width + norm_eps)
    normed_ref[...] = (residual_ref[...] * factor * gain_ref[...]).astype(jnp.bfloat16)


def expert_kernel(items, shape, aux_ref, *refs):
    nz, ny, nc = shape
    count = len(items)
    sources = refs[:count]
    weights = refs[count : count + 6]
    outs = refs[count + 6 : 2 * count + 6]
    x, aux, inner, gates, ups, down, x_sems, aux_sems, w_sems = refs[2 * count + 6 :]
    member, z, y, c, _ = own_place(shape)
    rows = outs[0].shape[0]
    width, hidden = weights[0].shape
    waits = []
    for i, (kz, ky) in enumerate(items):
        block = pl.ds(i * rows, rows)
        shard = ((z ^ kz) * ny + (y ^ ky)) * nc + c
        start = pl.multiple_of(shard * rows, rows)
        extra_rows = aux_ref.at[pl.ds(start, rows)]
        waits.append(pltpu.make_async_copy(sources[i], x.at[block], x_sems.at[i]))
        waits.append(pltpu.make_async_copy(extra_rows, aux.at[block], aux_sems.at[i]))
    targets = []
    for e in range(2):
        targets += [gates.at[e], ups.at[e]]
    targets += [down.at[pl.ds(0, hidden)], down.at[pl.ds(hidden, hidden)]]
    loads = [
        pltpu.make_async_copy(weights[i], targets[i], w_sems.at[i]) for i in range(len(targets))
    ]
    for copy in loads[:2] + waits + loads[2:]:
        copy.start()
    for wait in waits:
        wait.wait()
    extra = aux[...].astype(jnp.float32)
    lane = lax.broadcasted_iota(jnp.int32, extra.shape, 1)
    is_high = (lane >= HIGH_LANE) & (lane < HIGH_LANE + TOP)
    named = pltpu.roll(extra, HIGH_LANE - ROUTE_LANE, 1)
    share = extra + pltpu.roll(extra, LANES - (LOW_LANE - HIGH_LANE), 1)
    for e in range(2):
        expert = (member ^ e).astype(jnp.float32)
        chosen = lane_sum(jnp.where(is_high & (named == expert), share, 0.0))
        loads[2 * e].wait()
        gate = jnp.dot(x[...], gates[e], preferred_element_type=jnp.float32)
        loads[2 * e + 1].wait()
        up = jnp.dot(x[...], ups[e], preferred_element_type=jnp.float32)
        inner[:, e * hidden : (e + 1) * hidden] = (
            gate * jax.nn.sigmoid(gate) * up * chosen
        ).astype(jnp.bfloat16)
    loads[4].wait()
    loads[5].wait()
    step = 512
    for n in range(0, width, step):
        result = jnp.dot(inner[...], down[:, n : n + step], preferred_element_type=jnp.float32)
        for i in range(len(items)):
            outs[i][:, n : n + step] = result[i * rows : (i + 1) * rows].astype(jnp.bfloat16)


def body(
    dims,
    hidden_in,
    queries,
    keys_values,
    segment_ids,
    routes,
    gate_weights,
    page_table,
    out_weight,
    norm_gain,
    expert_gate,
    expert_up,
    expert_down,
):
    n_dp, nz, ny, nc = dims
    shape = (nz, ny, nc)
    members = nz * ny * nc
    tok_rows, width = hidden_in.shape
    member = lax.axis_index("expert")
    z, y, c = member // (ny * nc), member // nc % ny, member % nc
    params = pltpu.CompilerParams(vmem_limit_bytes=VMEM_LIMIT)

    def at(zz, yy, cc):
        return (zz * ny + yy) * nc + cc

    places = [(a, b, d) for a in range(nz) for b in range(ny) for d in range(nc)]

    def flip(array, kz, ky, kc):
        pairs = [(at(a, b, d), at(a ^ kz, b ^ ky, d ^ kc)) for a, b, d in places]
        return lax.ppermute(array, "expert", pairs)

    def move(array, hops):
        pairs = [(at(a, b, d), at(hops[a], b, d)) for a, b, d in places if a in hops]
        return lax.ppermute(array, "expert", pairs)

    def tie(first, *others):
        return lax.optimization_barrier((first, *others))

    slot_count = tok_rows // PAGE

    kv_cols = keys_values.shape[1]
    seg_row = segment_ids.reshape(1, tok_rows)
    packed = pl.pallas_call(
        pack_kernel,
        out_shape=jax.ShapeDtypeStruct((tok_rows, kv_cols + LANES), jnp.bfloat16),
        in_specs=[vmem_spec] * 4,
        out_specs=vmem_spec,
    )(keys_values, seg_row, routes.T, gate_weights.T)
    half = out_weight.shape[0]
    split_weight = n_dp == 2 and ny == 2 and nz == 4 and half % (8 * LANES) == 0
    got = []
    if split_weight:
        quarter = half // 4
        part = quarter // nc
        first = (y ^ (z & 1)) * 2 * quarter + c * part
        held_back, packed = tie(out_weight, packed)
        starts = (first, first + quarter)
        got = [lax.dynamic_slice_in_dim(held_back, start, part, 0) for start in starts]
        got[0] = lax.ppermute(got[0], "dp", [(0, 1), (1, 0)])
    along = [packed] + [flip(packed, kz, 0, 0) for kz in range(1, nz)]
    beside = [packed] + [flip(packed, 0, ky, 0) for ky in range(1, ny)]

    turned = pl.pallas_call(
        turn_kernel,
        out_shape=jax.ShapeDtypeStruct((HD, HQ * tok_rows), jnp.bfloat16),
        in_specs=[vmem_spec],
        out_specs=vmem_spec,
    )(queries)
    along, beside, turned, got = tie(along, beside, turned, got)
    if split_weight:
        got[1] = lax.ppermute(got[1], "dp", [(0, 1), (1, 0)])
    shards = {(kz, 0, 0): along[kz] for kz in range(nz)}
    shards.update({(0, ky, 0): beside[ky] for ky in range(1, ny)})
    near = list(shards)
    crossed = [(kz, ky, 0) for kz in range(1, nz) for ky in range(1, ny)]
    for kz, ky, _ in crossed:
        shards[kz, ky, 0] = flip(along[kz], 0, ky, 0)
    arrays, shards[crossed[0]] = tie([shards[name] for name in near], shards[crossed[0]])
    shards.update(zip(near, arrays))
    for kz, ky, _ in near:
        shards[kz, ky, 1] = flip(shards[kz, ky, 0], 0, 0, 1)
    shards = tie(shards)[0]
    for kz, ky, _ in crossed:
        shards[kz, ky, 1] = flip(shards[kz, ky, 0], 0, 0, 1)
    shard_list, got = tie([shards[place] for place in places], got)
    if split_weight:
        sent = [flip(got[0], 0, 1, 0), flip(got[1], 1, 0, 0)]
        got += [flip(array, 0, 0, 1) for array in got]
    own = [expert_gate[0], expert_up[0], expert_down[0]]
    own, shard_list = tie(own, shard_list)
    other = [flip(own[2], 0, 0, 1)]

    rest = half if split_weight else HQ * HD
    attended, partial, cache_pages, aux = pl.pallas_call(
        functools.partial(attend_kernel, shape, split_weight),
        out_shape=(
            jax.ShapeDtypeStruct((tok_rows, rest), jnp.bfloat16),
            jax.ShapeDtypeStruct((tok_rows, width), jnp.float32),
            jax.ShapeDtypeStruct((slot_count, PAGE, kv_cols), jnp.bfloat16),
            jax.ShapeDtypeStruct((members * tok_rows, LANES), jnp.bfloat16),
        ),
        in_specs=[smem_spec, vmem_spec, vmem_spec, vmem_spec] + [any_spec] * (1 + members),
        out_specs=(vmem_spec, vmem_spec, any_spec, any_spec),
        scratch_shapes=[
            pltpu.VMEM((members * tok_rows, kv_cols + LANES), jnp.bfloat16),
            pltpu.VMEM((1, HQ * tok_rows), jnp.float32),
            pltpu.VMEM((1, HQ * tok_rows), jnp.float32),
            pltpu.VMEM((HD, HQ * tok_rows), jnp.float32),
            pltpu.VMEM((tok_rows, HQ * HD), jnp.bfloat16),
            pltpu.VMEM(out_weight.shape, jnp.bfloat16),
            pltpu.SMEM((slot_count,), jnp.int32),
            pltpu.SemaphoreType.DMA((members,)),
            pltpu.SemaphoreType.DMA((2 + slot_count,)),
        ],
        compiler_params=params,
        cost_estimate=pl.CostEstimate(
            flops=ATTEND_COST, bytes_accessed=10**6, transcendentals=0
        ),
    )(page_table, seg_row, turned, hidden_in, out_weight, *shard_list)

    if split_weight:

        def from_other(turn, index, kc):
            def offset(pos):
                pair = pos[2] ^ (pos[1] & 1) ^ turn
                return (2 * pair + index) * quarter + (pos[3] ^ kc) * part

            return offset

        attended, sent, other = tie(attended, sent, other)
        pieces = got + sent + [flip(array, 0, 0, 1) for array in sent]
        offsets = [
            from_other(turn, index, kc) for turn in (0, 1) for kc in (0, 1) for index in (0, 1)
        ]
    else:
        pieces = [lax.all_gather(out_weight, "dp", axis=0, tiled=True)]
        offsets = [lambda pos: 0]
    residual, normed = pl.pallas_call(
        functools.partial(project_kernel, shape, offsets),
        out_shape=(
            jax.ShapeDtypeStruct((tok_rows, width), jnp.float32),
            jax.ShapeDtypeStruct((tok_rows, width), jnp.bfloat16),
        ),
        in_specs=[vmem_spec, vmem_spec, vmem_spec] + [any_spec] * len(pieces),
        out_specs=(vmem_spec, vmem_spec),
        scratch_shapes=[
            pltpu.VMEM((rest, width), jnp.bfloat16),
            pltpu.SemaphoreType.DMA((len(pieces),)),
        ],
        compiler_params=pltpu.CompilerParams(vmem_limit_bytes=20 * 1024 * 1024),
    )(attended, partial, norm_gain.reshape(1, width), *pieces)

    hidden = expert_gate.shape[2]
    results = {}
    blocks = {}

    def cross(k):
        for ky in range(1, ny):
            blocks[k, ky] = flip(blocks[k, 0], 0, ky, 0)

    def run_experts(items):
        for start in range(0, len(items), CALL_BLOCKS):
            run_call(items[start : start + CALL_BLOCKS])

    def run_call(items):
        rows = len(items) * tok_rows
        outs = pl.pallas_call(
            functools.partial(expert_kernel, items, shape),
            out_shape=[jax.ShapeDtypeStruct((tok_rows, width), jnp.bfloat16)] * len(items),
            in_specs=[any_spec] * (len(items) + 7),
            out_specs=[vmem_spec] * len(items),
            scratch_shapes=[
                pltpu.VMEM((rows, width), jnp.bfloat16),
                pltpu.VMEM((rows, LANES), jnp.bfloat16),
                pltpu.VMEM((rows, 2 * hidden), jnp.bfloat16),
                pltpu.VMEM((2, width, hidden), jnp.bfloat16),
                pltpu.VMEM((2, width, hidden), jnp.bfloat16),
                pltpu.VMEM((2 * hidden, width), jnp.bfloat16),
                pltpu.SemaphoreType.DMA((len(items),)),
                pltpu.SemaphoreType.DMA((len(items),)),
                pltpu.SemaphoreType.DMA((6,)),
            ],
            compiler_params=pltpu.CompilerParams(vmem_limit_bytes=24 * 1024 * 1024),
            cost_estimate=pl.CostEstimate(
                flops=EXPERT_COST,
                bytes_accessed=EXPERT_COST,
                transcendentals=0,
            ),
        )(aux, *[blocks[item] for item in items], *experts)
        results.update(zip(items, outs))

    own[:2], normed = tie(own[:2], normed)
    other = [flip(array, 0, 0, 1) for array in own[:2]] + other
    experts = [own[0], own[1], other[0], other[1], own[2], other[2]]
    blocks[0, 0] = normed
    relay = nz == 4
    inner = (z == 1) | (z == 2)
    hops = {}
    if relay:
        out, into, middles = {0: 1, 3: 2}, {1: 0, 2: 3}, {1: 2, 2: 1}
        hops[1] = flip(normed, 1, 0, 0)
        middle = move(normed, middles)
    for k in range(nz):
        if not relay and k > 0:
            blocks[k, 0] = flip(normed, k, 0, 0)
        elif k == 1:
            blocks[1, 0] = hops[1]
        elif k == 2:
            ends = move(middle, into)
            hops[2] = move(blocks[1, 0], middles)
            blocks[2, 0] = jnp.where(inner, hops[2], ends)
        elif k == 3:
            blocks[3, 0] = jnp.where(inner, middle, move(hops[2], into))
        if k > 0:
            before = [(k - 1, ky) for ky in range(1, ny)]
            blocks[k, 0], arrived = tie(blocks[k, 0], [blocks[item] for item in before])
            blocks.update(zip(before, arrived))
        cross(k)
        if k == nz - 2:
            late = [(k, ky) for ky in range(ny)] + [(k + 1, 0)]
    run_experts(late)
    across = [(nz - 1, ky) for ky in range(1, ny)]
    arrived, finished = tie(
        [blocks[item] for item in across], [results[item] for item in late]
    )
    blocks.update(zip(across, arrived))
    results.update(zip(late, finished))
    run_experts(across)
    early = [(k, ky) for k in range(nz - 2) for ky in range(ny)]
    blocks[0, 0], results[nz - 1, ny - 1] = tie(blocks[0, 0], results[nz - 1, ny - 1])
    run_experts(early)

    def as_float(array):
        return array.astype(jnp.float32)

    def back(k):
        return [flip(results[k, ky], 0, ky, 0) for ky in range(1, ny)]

    def total(k, arrived):
        value = as_float(results[k, 0])
        for array in arrived:
            value = value + as_float(array)
        return value

    def small(array):
        return array.astype(jnp.bfloat16)

    if relay:

        def next_back(k, arrived):
            items = [(k, ky) for ky in range(1, ny)]
            tied, arrived = tie([results[item] for item in items], arrived)
            results.update(zip(items, tied))
            return arrived, back(k)

        back3, finished = tie(back(3), [results[item] for item in early])
        results.update(zip(early, finished))
        back3, back2 = next_back(2, back3)
        third = total(3, back3)
        far = move(small(third), out)
        back2, back1 = next_back(1, back2)
        second = total(2, back2)
        far = move(small(second + as_float(far)), middles)
        near = move(small(second), out)
        back1, back0 = next_back(0, back1)
        far = flip(small(total(1, back1) + as_float(far)), 1, 0, 0)
        near = move(small(third + as_float(near)), middles)
        combined = total(0, back0) + as_float(far) + as_float(near)
    else:
        combined = total(0, back(0))
        for k in range(nz - 1, 0, -1):
            combined = combined + as_float(flip(small(total(k, back(k))), k, 0, 0))
    hidden_out = (residual + combined).astype(jnp.bfloat16)
    return (hidden_out, cache_pages)


def split_axis(mesh):
    n_dp = mesh.shape["dp"]
    members = mesh.shape["expert"]
    nc = 2
    ny = n_dp if members % (nc * n_dp) == 0 else 1
    return (n_dp, members // (nc * ny), ny, nc)


def solution(mesh):
    return jax.shard_map(
        functools.partial(body, split_axis(mesh)),
        mesh=mesh,
        in_specs=(
            P(("dp", "expert"), None),
            P(("dp", "expert"), None),
            P(("dp", "expert"), None),
            P("dp", "expert"),
            P(("dp", "expert"), None),
            P(("dp", "expert"), None),
            P("dp", None),
            P("dp", None),
            P(),
            P("expert", None, None),
            P("expert", None, None),
            P("expert", None, None),
        ),
        out_specs=(P(("dp", "expert"), None), P(("dp", "expert"), None, None)),
        check_vma=False,
    )
```

```python
import functools
import math

import jax
import jax.numpy as jnp
from jax import lax
from jax.experimental import pallas as pl
from jax.experimental.pallas import tpu as pltpu
from jax.sharding import PartitionSpec as P

HD = 128
HQ = 16
HK = 2
TOP = 8
PAGE = 16
LANES = 128
KEY_BLOCK = 256

neg_big = -1e30
norm_eps = 1e-06

ROUTE_LANE = 8
HIGH_LANE = 16
LOW_LANE = 24

VMEM_LIMIT = 60 * 1024 * 1024
CALL_BLOCKS = 4
EXPERT_COST = 10**6
ATTEND_COST = 10**6

vmem_spec = pl.BlockSpec(memory_space=pltpu.VMEM)
smem_spec = pl.BlockSpec(memory_space=pltpu.SMEM)
any_spec = pl.BlockSpec(memory_space=pltpu.HBM)


def own_place(shape):
    _, ny, nc = shape
    member = lax.axis_index("expert")
    return member, member // (ny * nc), member // nc % ny, member % nc, lax.axis_index("dp")


def lane_sum(values):
    return jnp.sum(values, axis=1, keepdims=True)


def pack_kernel(shape, kv_ref, seg_ref, routes_ref, weights_ref, *refs):
    copies = []
    if len(refs) > 1:
        matrix, out_ref, sems = refs[0], refs[1], refs[-1]
        _, z, y, c, _ = own_place(shape)
        part = refs[2].shape[0]
        pair = (y ^ (z & 1)) * 2
        for i, part_ref in enumerate(refs[2:-1]):
            start = pl.multiple_of(((pair + i) * shape[2] + c) * part, part)
            source = matrix.at[pl.ds(start, part)]
            copies.append(pltpu.make_async_copy(source, part_ref, sems.at[i]))
            copies[-1].start()
    else:
        out_ref = refs[0]
    rows, kv_cols = kv_ref.shape
    out_ref[:, :kv_cols] = kv_ref[...]
    row_id = lax.broadcasted_iota(jnp.int32, (rows, rows), 0)
    col_id = lax.broadcasted_iota(jnp.int32, (rows, rows), 1)
    identity = jnp.where(row_id == col_id, 1.0, 0.0).astype(jnp.bfloat16)
    weights = weights_ref[...]
    shares = weights / jnp.sum(weights, axis=0, keepdims=True)
    high = shares.astype(jnp.bfloat16).astype(jnp.float32)
    seg = jnp.broadcast_to(seg_ref[...].astype(jnp.float32), (ROUTE_LANE, rows))
    lines = [seg, routes_ref[...].astype(jnp.float32), high, shares - high]
    lines.append(jnp.zeros((LANES - LOW_LANE - TOP, rows), jnp.float32))
    lines = jnp.concatenate(lines, axis=0).astype(jnp.bfloat16)
    turned = lax.dot_general(
        identity, lines, (((1,), (1,)), ((), ())), preferred_element_type=jnp.float32
    )
    out_ref[:, kv_cols:] = turned.astype(jnp.bfloat16)
    for copy in copies:
        copy.wait()


def turn_kernel(q_ref, out_ref):
    rows = q_ref.shape[0]
    for h in range(HQ):
        part = q_ref[:, h * HD : (h + 1) * HD].astype(jnp.float32)
        out_ref[:, h * rows : (h + 1) * rows] = part.T.astype(jnp.bfloat16)


def attend_kernel(shape, own_part, table_ref, seg_ref, q_ref, hidden_ref, weight_ref, *refs):
    nz, ny, nc = shape
    count = nz * ny * nc
    shards = refs[:count]
    out_ref, partial_ref, cache_ref, aux_ref = refs[count : count + 4]
    held, top, total, acc, attended, weight, pages, sems, more_sems = refs[count + 4 :]
    tok_rows, width = hidden_ref.shape
    kv_width = HK * HD
    member, z, y, c, side = own_place(shape)
    copies = []
    for i in range(count):
        kz, ky, kc = i // (ny * nc), i // nc % ny, i % nc
        shard = ((z ^ kz) * ny + (y ^ ky)) * nc + (c ^ kc)
        start = pl.multiple_of(shard * tok_rows, tok_rows)
        copy = pltpu.make_async_copy(shards[i], held.at[pl.ds(start, tok_rows)], sems.at[i])
        copy.start()
        copies.append(copy)
    weight_copy = pltpu.make_async_copy(weight_ref, weight, more_sems.at[0])
    if own_part:
        weight_copy.start()
    top[...] = jnp.full(top.shape, neg_big, jnp.float32)
    total[...] = jnp.zeros(total.shape, jnp.float32)
    acc[...] = jnp.zeros(acc.shape, jnp.float32)
    slots = cache_ref.shape[0]

    def find_slot(page, carried):
        slot = table_ref[0, page] - member * slots

        @pl.when((slot >= 0) & (slot < slots))
        def _():
            pages[slot] = page

        return carried

    lax.fori_loop(0, table_ref.shape[1], find_slot, 0, unroll=8)
    for copy in copies:
        copy.wait()
    later = [pltpu.make_async_copy(held.at[:, 2 * kv_width :], aux_ref, more_sems.at[1])]
    for s in range(slots):
        start = pl.multiple_of(pages[s] * PAGE, PAGE)
        page = held.at[pl.ds(start, PAGE), pl.ds(0, 2 * kv_width)]
        later.append(pltpu.make_async_copy(page, cache_ref.at[s], more_sems.at[2 + s]))
    for copy in later:
        copy.start()
    own_seg = seg_ref[...].astype(jnp.float32)

    def count_lower(s, below):
        start = pl.multiple_of(s * tok_rows, tok_rows)
        seg = held[pl.ds(start, tok_rows), 2 * kv_width :][:, 0:1].astype(jnp.float32)
        return below + jnp.where(seg < own_seg, 1.0, 0.0)

    below = lax.fori_loop(0, member + 1, count_lower, jnp.zeros((tok_rows, tok_rows), jnp.float32))
    seg_start = jnp.sum(below, axis=0, keepdims=True).astype(jnp.int32)
    first_row = member * tok_rows
    query_pos = first_row + lax.broadcasted_iota(jnp.int32, (1, tok_rows), 1)
    last_block = first_row // KEY_BLOCK
    first_block = jnp.min(seg_start) // KEY_BLOCK
    scale = 1.0 / math.sqrt(HD)
    heads = 4
    cols = heads * tok_rows
    groups = HQ // HK

    def attend(step, carried):
        base = pl.multiple_of((last_block - step) * KEY_BLOCK, KEY_BLOCK)
        key_pos = base + lax.broadcasted_iota(jnp.int32, (KEY_BLOCK, tok_rows), 0)
        seen = (key_pos >= seg_start) & (key_pos <= query_pos)
        bias = jnp.where(seen, 0.0, neg_big)
        bias = jnp.concatenate([bias] * heads, axis=1)
        units = [
            (g, slice((g * groups + u) * tok_rows, (g * groups + u) * tok_rows + cols))
            for g in range(HK)
            for u in range(0, groups, heads)
        ]
        keys = [held[pl.ds(base, KEY_BLOCK), g * HD : (g + 1) * HD] for g in range(HK)]
        values = []
        for g in range(HK):
            value = held[pl.ds(base, KEY_BLOCK), kv_width + g * HD : kv_width + (g + 1) * HD]
            values.append(value.astype(jnp.float32).T.astype(jnp.bfloat16))
        scores = [
            jnp.dot(keys[g], q_ref[:, unit], preferred_element_type=jnp.float32) + bias
            for g, unit in units
        ]
        old_tops = [top[:, unit] for _, unit in units]
        new_tops = [
            jnp.maximum(old, jnp.max(score, axis=0, keepdims=True))
            for old, score in zip(old_tops, scores)
        ]
        weights = [jnp.exp((score - new) * scale) for score, new in zip(scores, new_tops)]
        added = [
            jnp.dot(values[g], weight.astype(jnp.bfloat16), preferred_element_type=jnp.float32)
            for (g, _), weight in zip(units, weights)
        ]
        for i, (_, unit) in enumerate(units):
            factor = jnp.exp((old_tops[i] - new_tops[i]) * scale)
            top[:, unit] = new_tops[i]
            sums = jnp.sum(weights[i], axis=0, keepdims=True)
            total[:, unit] = total[:, unit] * factor + sums
            acc[:, unit] = acc[:, unit] * factor + added[i]
        return carried

    lax.fori_loop(0, last_block - first_block + 1, attend, 0)
    for h in range(HQ):
        unit = slice(h * tok_rows, (h + 1) * tok_rows)
        head = acc[:, unit] / total[:, unit]
        attended[:, h * HD : (h + 1) * HD] = head.T.astype(jnp.bfloat16)
    step = 512
    if own_part:
        half = weight.shape[0]
        mine = attended[:, pl.ds(pl.multiple_of(side * half, half), half)]
        out_ref[...] = attended[:, pl.ds(pl.multiple_of((1 - side) * half, half), half)]
        weight_copy.wait()
        for n in range(0, width, step):
            part = slice(n, n + step)
            partial_ref[:, part] = hidden_ref[:, part].astype(jnp.float32) + jnp.dot(
                mine, weight[:, part], preferred_element_type=jnp.float32
            )
    else:
        out_ref[...] = attended[...]
        partial_ref[...] = hidden_ref[...].astype(jnp.float32)
    for copy in later:
        copy.wait()


def project_kernel(shape, offsets, att_ref, partial_ref, gain_ref, *refs):
    count = len(offsets)
    pieces = refs[:count]
    residual_ref, normed_ref, weight, sems = refs[count:]
    rows, width = partial_ref.shape
    copies = []
    for i in range(count):
        piece_rows = pieces[i].shape[0]
        start = pl.multiple_of(offsets[i](own_place(shape)), LANES)
        copy = pltpu.make_async_copy(pieces[i], weight.at[pl.ds(start, piece_rows)], sems.at[i])
        copy.start()
        copies.append(copy)
    for copy in copies:
        copy.wait()
    step = 512
    squares = jnp.zeros((rows, 1), jnp.float32)
    for n in range(0, width, step):
        cols = slice(n, n + step)
        projected = jnp.dot(att_ref[...], weight[:, cols], preferred_element_type=jnp.float32)
        part = partial_ref[:, cols] + projected
        residual_ref[:, cols] = part
        squares = squares + lane_sum(part * part)
    factor = lax.rsqrt(squares / width + norm_eps)
    normed_ref[...] = (residual_ref[...] * factor * gain_ref[...]).astype(jnp.bfloat16)


def expert_kernel(items, shape, aux_ref, *refs):
    nz, ny, nc = shape
    count = len(items)
    sources = refs[:count]
    weights = refs[count : count + 6]
    outs = refs[count + 6 : 2 * count + 6]
    x, aux, inner, gates, ups, down, x_sems, aux_sems, w_sems = refs[2 * count + 6 :]
    member, z, y, c, _ = own_place(shape)
    rows = outs[0].shape[0]
    width, hidden = weights[0].shape
    waits = []
    for i, (kz, ky) in enumerate(items):
        block = pl.ds(i * rows, rows)
        shard = ((z ^ kz) * ny + (y ^ ky)) * nc + c
        start = pl.multiple_of(shard * rows, rows)
        extra_rows = aux_ref.at[pl.ds(start, rows)]
        waits.append(pltpu.make_async_copy(sources[i], x.at[block], x_sems.at[i]))
        waits.append(pltpu.make_async_copy(extra_rows, aux.at[block], aux_sems.at[i]))
    targets = []
    for e in range(2):
        targets += [gates.at[e], ups.at[e]]
    targets += [down.at[pl.ds(0, hidden)], down.at[pl.ds(hidden, hidden)]]
    loads = [
        pltpu.make_async_copy(weights[i], targets[i], w_sems.at[i]) for i in range(len(targets))
    ]
    for copy in loads[:2] + waits + loads[2:]:
        copy.start()
    for wait in waits:
        wait.wait()
    extra = aux[...].astype(jnp.float32)
    lane = lax.broadcasted_iota(jnp.int32, extra.shape, 1)
    is_high = (lane >= HIGH_LANE) & (lane < HIGH_LANE + TOP)
    named = pltpu.roll(extra, HIGH_LANE - ROUTE_LANE, 1)
    share = extra + pltpu.roll(extra, LANES - (LOW_LANE - HIGH_LANE), 1)
    for e in range(2):
        expert = (member ^ e).astype(jnp.float32)
        chosen = lane_sum(jnp.where(is_high & (named == expert), share, 0.0))
        loads[2 * e].wait()
        gate = jnp.dot(x[...], gates[e], preferred_element_type=jnp.float32)
        loads[2 * e + 1].wait()
        up = jnp.dot(x[...], ups[e], preferred_element_type=jnp.float32)
        inner[:, e * hidden : (e + 1) * hidden] = (
            gate * jax.nn.sigmoid(gate) * up * chosen
        ).astype(jnp.bfloat16)
    loads[4].wait()
    loads[5].wait()
    step = 512
    for n in range(0, width, step):
        result = jnp.dot(inner[...], down[:, n : n + step], preferred_element_type=jnp.float32)
        for i in range(len(items)):
            outs[i][:, n : n + step] = result[i * rows : (i + 1) * rows].astype(jnp.bfloat16)


def body(
    dims,
    hidden_in,
    queries,
    keys_values,
    segment_ids,
    routes,
    gate_weights,
    page_table,
    out_weight,
    norm_gain,
    expert_gate,
    expert_up,
    expert_down,
):
    n_dp, nz, ny, nc = dims
    shape = (nz, ny, nc)
    members = nz * ny * nc
    tok_rows, width = hidden_in.shape
    member = lax.axis_index("expert")
    z, y, c = member // (ny * nc), member // nc % ny, member % nc
    params = pltpu.CompilerParams(vmem_limit_bytes=VMEM_LIMIT)

    def at(zz, yy, cc):
        return (zz * ny + yy) * nc + cc

    places = [(a, b, d) for a in range(nz) for b in range(ny) for d in range(nc)]

    def flip(array, kz, ky, kc):
        pairs = [(at(a, b, d), at(a ^ kz, b ^ ky, d ^ kc)) for a, b, d in places]
        return lax.ppermute(array, "expert", pairs)

    def move(array, hops):
        pairs = [(at(a, b, d), at(hops[a], b, d)) for a, b, d in places if a in hops]
        return lax.ppermute(array, "expert", pairs)

    def tie(first, *others):
        return lax.optimization_barrier((first, *others))

    slot_count = tok_rows // PAGE

    kv_cols = keys_values.shape[1]
    seg_row = segment_ids.reshape(1, tok_rows)
    half = out_weight.shape[0]
    split_weight = n_dp == 2 and ny == 2 and nz == 4 and half % (8 * LANES) == 0
    quarter = half // 4
    part = quarter // nc
    parts = [jax.ShapeDtypeStruct((part, width), jnp.bfloat16)] * (2 * split_weight)
    packed, *got = pl.pallas_call(
        functools.partial(pack_kernel, shape),
        out_shape=[jax.ShapeDtypeStruct((tok_rows, kv_cols + LANES), jnp.bfloat16)] + parts,
        in_specs=[vmem_spec] * 4 + [any_spec] * split_weight,
        out_specs=[vmem_spec] * (1 + len(parts)),
        scratch_shapes=[pltpu.SemaphoreType.DMA((2,))] * split_weight,
    )(keys_values, seg_row, routes.T, gate_weights.T, *[out_weight] * split_weight)
    if split_weight:
        got[0] = lax.ppermute(got[0], "dp", [(0, 1), (1, 0)])
    along = [packed] + [flip(packed, kz, 0, 0) for kz in range(1, nz)]
    beside = [packed] + [flip(packed, 0, ky, 0) for ky in range(1, ny)]

    turned = pl.pallas_call(
        turn_kernel,
        out_shape=jax.ShapeDtypeStruct((HD, HQ * tok_rows), jnp.bfloat16),
        in_specs=[vmem_spec],
        out_specs=vmem_spec,
    )(queries)
    along, beside, turned, got = tie(along, beside, turned, got)
    if split_weight:
        got[1] = lax.ppermute(got[1], "dp", [(0, 1), (1, 0)])
    shards = {(kz, 0, 0): along[kz] for kz in range(nz)}
    shards.update({(0, ky, 0): beside[ky] for ky in range(1, ny)})
    near = list(shards)
    crossed = [(kz, ky, 0) for kz in range(1, nz) for ky in range(1, ny)]
    for kz, ky, _ in crossed:
        shards[kz, ky, 0] = flip(along[kz], 0, ky, 0)
    arrays, shards[crossed[0]] = tie([shards[name] for name in near], shards[crossed[0]])
    shards.update(zip(near, arrays))
    for kz, ky, _ in near:
        shards[kz, ky, 1] = flip(shards[kz, ky, 0], 0, 0, 1)
    shards = tie(shards)[0]
    for kz, ky, _ in crossed:
        shards[kz, ky, 1] = flip(shards[kz, ky, 0], 0, 0, 1)
    shard_list, got = tie([shards[place] for place in places], got)
    if split_weight:
        sent = [flip(got[0], 0, 1, 0), flip(got[1], 1, 0, 0)]
        got += [flip(array, 0, 0, 1) for array in got]
    own = [expert_gate[0], expert_up[0], expert_down[0]]
    own, shard_list = tie(own, shard_list)
    other = [flip(own[2], 0, 0, 1)]

    rest = half if split_weight else HQ * HD
    attended, partial, cache_pages, aux = pl.pallas_call(
        functools.partial(attend_kernel, shape, split_weight),
        out_shape=(
            jax.ShapeDtypeStruct((tok_rows, rest), jnp.bfloat16),
            jax.ShapeDtypeStruct((tok_rows, width), jnp.float32),
            jax.ShapeDtypeStruct((slot_count, PAGE, kv_cols), jnp.bfloat16),
            jax.ShapeDtypeStruct((members * tok_rows, LANES), jnp.bfloat16),
        ),
        in_specs=[smem_spec, vmem_spec, vmem_spec, vmem_spec] + [any_spec] * (1 + members),
        out_specs=(vmem_spec, vmem_spec, any_spec, any_spec),
        scratch_shapes=[
            pltpu.VMEM((members * tok_rows, kv_cols + LANES), jnp.bfloat16),
            pltpu.VMEM((1, HQ * tok_rows), jnp.float32),
            pltpu.VMEM((1, HQ * tok_rows), jnp.float32),
            pltpu.VMEM((HD, HQ * tok_rows), jnp.float32),
            pltpu.VMEM((tok_rows, HQ * HD), jnp.bfloat16),
            pltpu.VMEM(out_weight.shape, jnp.bfloat16),
            pltpu.SMEM((slot_count,), jnp.int32),
            pltpu.SemaphoreType.DMA((members,)),
            pltpu.SemaphoreType.DMA((2 + slot_count,)),
        ],
        compiler_params=params,
        cost_estimate=pl.CostEstimate(
            flops=ATTEND_COST, bytes_accessed=10**6, transcendentals=0
        ),
    )(page_table, seg_row, turned, hidden_in, out_weight, *shard_list)

    if split_weight:

        def from_other(turn, index, kc):
            def offset(pos):
                pair = pos[2] ^ (pos[1] & 1) ^ turn
                return (2 * pair + index) * quarter + (pos[3] ^ kc) * part

            return offset

        attended, sent, other = tie(attended, sent, other)
        pieces = got + sent + [flip(array, 0, 0, 1) for array in sent]
        offsets = [
            from_other(turn, index, kc) for turn in (0, 1) for kc in (0, 1) for index in (0, 1)
        ]
    else:
        pieces = [lax.all_gather(out_weight, "dp", axis=0, tiled=True)]
        offsets = [lambda pos: 0]
    residual, normed = pl.pallas_call(
        functools.partial(project_kernel, shape, offsets),
        out_shape=(
            jax.ShapeDtypeStruct((tok_rows, width), jnp.float32),
            jax.ShapeDtypeStruct((tok_rows, width), jnp.bfloat16),
        ),
        in_specs=[vmem_spec, vmem_spec, vmem_spec] + [any_spec] * len(pieces),
        out_specs=(vmem_spec, vmem_spec),
        scratch_shapes=[
            pltpu.VMEM((rest, width), jnp.bfloat16),
            pltpu.SemaphoreType.DMA((len(pieces),)),
        ],
        compiler_params=pltpu.CompilerParams(vmem_limit_bytes=20 * 1024 * 1024),
    )(attended, partial, norm_gain.reshape(1, width), *pieces)

    hidden = expert_gate.shape[2]
    results = {}
    blocks = {}

    def cross(k):
        for ky in range(1, ny):
            blocks[k, ky] = flip(blocks[k, 0], 0, ky, 0)

    def run_experts(items):
        for start in range(0, len(items), CALL_BLOCKS):
            run_call(items[start : start + CALL_BLOCKS])

    def run_call(items):
        rows = len(items) * tok_rows
        outs = pl.pallas_call(
            functools.partial(expert_kernel, items, shape),
            out_shape=[jax.ShapeDtypeStruct((tok_rows, width), jnp.bfloat16)] * len(items),
            in_specs=[any_spec] * (len(items) + 7),
            out_specs=[vmem_spec] * len(items),
            scratch_shapes=[
                pltpu.VMEM((rows, width), jnp.bfloat16),
                pltpu.VMEM((rows, LANES), jnp.bfloat16),
                pltpu.VMEM((rows, 2 * hidden), jnp.bfloat16),
                pltpu.VMEM((2, width, hidden), jnp.bfloat16),
                pltpu.VMEM((2, width, hidden), jnp.bfloat16),
                pltpu.VMEM((2 * hidden, width), jnp.bfloat16),
                pltpu.SemaphoreType.DMA((len(items),)),
                pltpu.SemaphoreType.DMA((len(items),)),
                pltpu.SemaphoreType.DMA((6,)),
            ],
            compiler_params=pltpu.CompilerParams(vmem_limit_bytes=24 * 1024 * 1024),
            cost_estimate=pl.CostEstimate(
                flops=EXPERT_COST,
                bytes_accessed=EXPERT_COST,
                transcendentals=0,
            ),
        )(aux, *[blocks[item] for item in items], *experts)
        results.update(zip(items, outs))

    own[:2], normed = tie(own[:2], normed)
    other = [flip(array, 0, 0, 1) for array in own[:2]] + other
    experts = [own[0], own[1], other[0], other[1], own[2], other[2]]
    blocks[0, 0] = normed
    relay = nz == 4
    inner = (z == 1) | (z == 2)
    hops = {}
    if relay:
        out, into, middles = {0: 1, 3: 2}, {1: 0, 2: 3}, {1: 2, 2: 1}
        hops[1] = flip(normed, 1, 0, 0)
        middle = move(normed, middles)
    for k in range(nz):
        if not relay and k > 0:
            blocks[k, 0] = flip(normed, k, 0, 0)
        elif k == 1:
            blocks[1, 0] = hops[1]
        elif k == 2:
            ends = move(middle, into)
            hops[2] = move(blocks[1, 0], middles)
            blocks[2, 0] = jnp.where(inner, hops[2], ends)
        elif k == 3:
            blocks[3, 0] = jnp.where(inner, middle, move(hops[2], into))
        if k > 0:
            before = [(k - 1, ky) for ky in range(1, ny)]
            blocks[k, 0], arrived = tie(blocks[k, 0], [blocks[item] for item in before])
            blocks.update(zip(before, arrived))
        cross(k)
        if k == nz - 2:
            late = [(k, ky) for ky in range(ny)] + [(k + 1, 0)]
    run_experts(late)
    across = [(nz - 1, ky) for ky in range(1, ny)]
    arrived, finished = tie(
        [blocks[item] for item in across], [results[item] for item in late]
    )
    blocks.update(zip(across, arrived))
    results.update(zip(late, finished))
    run_experts(across)
    early = [(k, ky) for k in range(nz - 2) for ky in range(ny)]
    blocks[0, 0], results[nz - 1, ny - 1] = tie(blocks[0, 0], results[nz - 1, ny - 1])
    run_experts(early)

    def as_float(array):
        return array.astype(jnp.float32)

    def back(k):
        return [flip(results[k, ky], 0, ky, 0) for ky in range(1, ny)]

    def total(k, arrived):
        value = as_float(results[k, 0])
        for array in arrived:
            value = value + as_float(array)
        return value

    def small(array):
        return array.astype(jnp.bfloat16)

    if relay:

        def next_back(k, arrived):
            items = [(k, ky) for ky in range(1, ny)]
            tied, arrived = tie([results[item] for item in items], arrived)
            results.update(zip(items, tied))
            return arrived, back(k)

        back3, finished = tie(back(3), [results[item] for item in early])
        results.update(zip(early, finished))
        back3, back2 = next_back(2, back3)
        third = total(3, back3)
        far = move(small(third), out)
        back2, back1 = next_back(1, back2)
        second = total(2, back2)
        far = move(small(second + as_float(far)), middles)
        near = move(small(second), out)
        back1, back0 = next_back(0, back1)
        far = flip(small(total(1, back1) + as_float(far)), 1, 0, 0)
        near = move(small(third + as_float(near)), middles)
        combined = total(0, back0) + as_float(far) + as_float(near)
    else:
        combined = total(0, back(0))
        for k in range(nz - 1, 0, -1):
            combined = combined + as_float(flip(small(total(k, back(k))), k, 0, 0))
    hidden_out = (residual + combined).astype(jnp.bfloat16)
    return (hidden_out, cache_pages)


def split_axis(mesh):
    n_dp = mesh.shape["dp"]
    members = mesh.shape["expert"]
    nc = 2
    ny = n_dp if members % (nc * n_dp) == 0 else 1
    return (n_dp, members // (nc * ny), ny, nc)


def solution(mesh):
    return jax.shard_map(
        functools.partial(body, split_axis(mesh)),
        mesh=mesh,
        in_specs=(
            P(("dp", "expert"), None),
            P(("dp", "expert"), None),
            P(("dp", "expert"), None),
            P("dp", "expert"),
            P(("dp", "expert"), None),
            P(("dp", "expert"), None),
            P("dp", None),
            P("dp", None),
            P(),
            P("expert", None, None),
            P("expert", None, None),
            P("expert", None, None),
        ),
        out_specs=(P(("dp", "expert"), None), P(("dp", "expert"), None, None)),
        check_vma=False,
    )
```
